128 devices in a mesh: row: 16 (over x, z), col: 8 (over y, core).
Axes of the slice: x: 4, y: 4, z: 4, core: 2. Of those that a mesh axis runs over, the one named last changes fastest.
Arguments:
- query_tiles: bfloat16 [512, 512, 512], P('row', 'col'), may hold values from -12 to 12
- key_tiles: bfloat16 [512, 512, 512], P('row', 'col'), may hold values from -12 to 12
- value_tiles: bfloat16 [512, 512, 512], P('row', 'col'), may hold values from -6 to 6
- out_grad: bfloat16 [512, 512, 512], P('row', 'col'), may hold values from -6 to 6
Outputs:
- attended: bfloat16 [512, 512, 512], P('row', 'col')
- query_grad: bfloat16 [512, 512, 512], P('row', 'col')
- key_grad: bfloat16 [512, 512, 512], P('row', 'col')
- value_grad: bfloat16 [512, 512, 512], P('row', 'col')
The draws below stay inside these ranges and needn't reach their ends.
All inputs are finite; a program needn't handle non-finite values.
Results may differ from the reference program's by a relative error of at most 0.015.
Values may be sent and summed in bfloat16 or wider, within the bound.
A program may use at most 192 MiB of HBM per device.

```python
from functools import partial
import jax
import jax.numpy as jnp
from jax import lax

G = 512
H = 4
E = 128


def base_field(key):
    return jnp.clip(jax.random.normal(key, (G, G, H * E), jnp.float32), -6.0, 6.0)


def draw_query_tiles(key, part):
    values_field = base_field(jax.random.fold_in(key, 1))
    return values_field.astype(jnp.bfloat16)


def draw_key_tiles(key, part):
    values_field = base_field(jax.random.fold_in(key, 2))
    return values_field.astype(jnp.bfloat16)


def block_levels(rng, dims, pieces, smallest, high):
    factor_of = 1.0
    for dim, shards_of in pieces:
        draws = jax.random.uniform(jax.random.fold_in(jax.random.fold_in(rng, 6), dim), (shards_of,), jnp.float32, smallest / len(pieces), high / len(pieces))
        factor_of = factor_of * jnp.repeat(jnp.exp(draws), dims[dim] // shards_of).reshape((-1,) + (1,) * (len(dims) - 1 - dim))
    return factor_of


def noise(rng, shape, spread, most, split=(), kind=jnp.bfloat16):
    values = spread * jax.random.normal(rng, shape, jnp.float32)
    if split:
        values = values * block_levels(rng, shape, split, -0.22, 0.18)
    return jnp.clip(values, -most, most).astype(kind)


def setup_inputs(seed: int = 0) -> dict:
    streams_of = jax.random.split(jax.random.key(seed), 5)
    query_tiles = draw_query_tiles(jax.random.fold_in(streams_of[4], 71), 0)
    key_tiles = draw_key_tiles(jax.random.fold_in(streams_of[4], 71), 0)
    value_tiles = noise(streams_of[2], (G, G, H * E), 1.0, 6.0, ((0, 16), (1, 8)))
    out_grad = noise(streams_of[3], (G, G, H * E), 1.0, 6.0, ((0, 16), (1, 8)))
    return dict(query_tiles=query_tiles, key_tiles=key_tiles, value_tiles=value_tiles, out_grad=out_grad)


NEG_FILL = -1.0e30


def round_half(values_in):
    return lax.optimization_barrier(values_in.astype(jnp.bfloat16)).astype(jnp.float32)


def causal_mask(length, strict):
    query_pos = lax.broadcasted_iota(jnp.int32, (length, length), 0)
    key_pos = lax.broadcasted_iota(jnp.int32, (length, length), 1)
    if strict:
        return key_pos < query_pos
    return key_pos <= query_pos


def split_heads(array_in):
    return array_in.astype(jnp.float32).reshape(array_in.shape[0], G, H, E)


def part_forward(query_rows, key_rows, value_rows, strict):
    batch_count = query_rows.shape[0]
    query_heads = split_heads(query_rows)
    key_heads = split_heads(key_rows)
    value_heads = split_heads(value_rows)
    scores = jnp.einsum("bqhe,bkhe->bhqk", query_heads, key_heads) * (E ** -0.5)
    causal = causal_mask(G, strict)
    top_score = jnp.max(jnp.where(causal, scores, NEG_FILL), axis=-1)
    weights = jnp.where(causal, jnp.exp(scores - top_score[..., None]), 0.0)
    weight_sum = jnp.maximum(jnp.sum(weights, axis=-1), 1.0)
    numerator = jnp.einsum("bhqk,bkhe->bqhe", round_half(weights), value_heads)
    partial_out = numerator / jnp.transpose(weight_sum, (0, 2, 1))[..., None]
    log_total = jnp.transpose(top_score + jnp.log(weight_sum), (0, 2, 1))
    return partial_out.reshape(batch_count, G, H * E).astype(jnp.bfloat16), log_total


def part_backward(query_rows, key_rows, value_rows, grad_rows, log_total, grad_dot, strict):
    batch_count = query_rows.shape[0]
    query_heads = split_heads(query_rows)
    key_heads = split_heads(key_rows)
    value_heads = split_heads(value_rows)
    grad_heads = split_heads(grad_rows)
    scale_factor = E ** -0.5
    scores = jnp.einsum("bqhe,bkhe->bhqk", query_heads, key_heads) * scale_factor
    causal = causal_mask(G, strict)
    total_back = jnp.transpose(log_total, (0, 2, 1))
    weights = jnp.where(causal, jnp.exp(scores - total_back[..., None]), 0.0)
    weight_grad = jnp.einsum("bqhe,bkhe->bhqk", grad_heads, value_heads)
    score_grad = weights * (weight_grad - jnp.transpose(grad_dot, (0, 2, 1))[..., None])
    weights_half = round_half(weights)
    score_half = round_half(score_grad)
    value_grad = jnp.einsum("bhqk,bqhe->bkhe", weights_half, grad_heads)
    query_grad = jnp.einsum("bhqk,bkhe->bqhe", score_half, key_heads) * scale_factor
    key_grad = jnp.einsum("bhqk,bqhe->bkhe", score_half, query_heads) * scale_factor
    return (query_grad.reshape(batch_count, G, H * E).astype(jnp.bfloat16),
            key_grad.reshape(batch_count, G, H * E).astype(jnp.bfloat16),
            value_grad.reshape(batch_count, G, H * E).astype(jnp.bfloat16))


def blockwise(function, arrays):
    shaped = tuple(array_in.reshape((G // 16, 16) + array_in.shape[1:]) for array_in in arrays)
    outcome = lax.map(lambda grouped_in: function(*grouped_in), shaped)
    return tuple(result.reshape((G,) + result.shape[2:]) for result in outcome)


def reference(query_tiles, key_tiles, value_tiles, out_grad):
    out_row, total_row = blockwise(partial(part_forward, strict=False), (query_tiles, key_tiles, value_tiles))
    swapped = tuple(jnp.swapaxes(array_in, 0, 1) for array_in in (query_tiles, key_tiles, value_tiles, out_grad))
    out_col, total_col = blockwise(partial(part_forward, strict=True), swapped[:3])
    total_col_t = jnp.swapaxes(total_col, 0, 1)
    top_total = jnp.maximum(total_row, total_col_t)
    log_total = top_total + jnp.log(jnp.exp(total_row - top_total) + jnp.exp(total_col_t - top_total))
    share_row = jnp.exp(total_row - log_total)
    share_col = jnp.exp(total_col_t - log_total)
    part_row = out_row.astype(jnp.float32).reshape(G, G, H, E)
    part_col = jnp.swapaxes(out_col, 0, 1).astype(jnp.float32).reshape(G, G, H, E)
    weighted_row = round_half(share_row[..., None] * part_row)
    weighted_col = round_half(share_col[..., None] * part_col)
    attended = (weighted_row + weighted_col).reshape(G, G, H * E).astype(jnp.bfloat16)
    merged = share_row[..., None] * part_row + share_col[..., None] * part_col
    grad_dot = jnp.sum(out_grad.astype(jnp.float32).reshape(G, G, H, E) * merged, axis=-1)
    grads_row = blockwise(partial(part_backward, strict=False),
                          (query_tiles, key_tiles, value_tiles, out_grad, log_total, grad_dot))
    grads_col = blockwise(partial(part_backward, strict=True),
                          swapped + (jnp.swapaxes(log_total, 0, 1), jnp.swapaxes(grad_dot, 0, 1)))
    summed = tuple((grads_row[member].astype(jnp.float32)
                    + jnp.swapaxes(grads_col[member], 0, 1).astype(jnp.float32)).astype(jnp.bfloat16)
                   for member in range(3))
    return attended, summed[0], summed[1], summed[2]
```

```python
import functools

import jax
import jax.numpy as jnp
from jax import lax
from jax.experimental import pallas as pl
from jax.experimental.pallas import tpu as pltpu
from jax.sharding import PartitionSpec as P

H = 4
E = 128
G = 512
ROWS = 32
COLS = 64
NR = 16
NC = 8
K = 4
HALF = 256
LOG2E = 1.4426950408889634
SCALE = E ** (-0.5)
NEG = -1e30
MESH = pl.DeviceIdType.MESH
F32 = jnp.float32
BF16 = jnp.bfloat16


def dot_nn(a, b):
    return lax.dot_general(a, b, (((1,), (0,)), ((), ())), preferred_element_type=F32)


def dot_nt(a, b):
    return lax.dot_general(a, b, (((1,), (1,)), ((), ())), preferred_element_type=F32)


def dot_tn(a, b):
    return lax.dot_general(a, b, (((0,), (0,)), ((), ())), preferred_element_type=F32)


def swap_matrix():
    to = lax.broadcasted_iota(jnp.int32, (HALF, HALF), 0)
    of = lax.broadcasted_iota(jnp.int32, (HALF, HALF), 1)
    match = of == (to % 16) * 16 + to // 16
    return jnp.where(match, 1.0, 0.0).astype(BF16)


def kernel(
    q_in, k_in, v_in, g_in, row_back, col_back,
    xs, xt, ab, perm, st, so, rs, cs, mr, mc, rr, cr, mm, pr, pc, ct, lt,
    load_sem, in_send, in_recv, out_send, out_recv, stat_send, stat_recv, merged_send, merged_recv,
):
    me_r = lax.axis_index("row")
    me_c = lax.axis_index("col")
    core = lax.rem(me_c, 2)
    me_z = lax.rem(me_r, 4)
    inputs = (q_in, k_in, v_in, g_in)

    def row_peer(d):
        return lax.rem(me_c + d, NC)

    def col_peer(d):
        return lax.rem(me_r + d, NR)

    def load(h):
        return [
            pltpu.make_async_copy(
                inputs[a].at[:, :, pl.ds(pl.multiple_of(h * E, E), E)], xs.at[h, a], load_sem.at[h, a]
            )
            for a in range(4)
        ]

    for h in range(H):
        for copy in load(h):
            copy.start()

    barrier = pltpu.get_barrier_semaphore()

    @pl.loop(1, NC)
    def _(d):
        pl.semaphore_signal(barrier, inc=1, device_id=(me_r, row_peer(d)), device_id_type=MESH)

    @pl.loop(1, NR)
    def _(d):
        pl.semaphore_signal(barrier, inc=1, device_id=(col_peer(d), me_c), device_id_type=MESH)

    perm[...] = swap_matrix()
    st[...] = jnp.zeros_like(st)
    lt[...] = jnp.zeros_like(lt)
    pl.semaphore_wait(barrier, NC + NR - 2)

    def send_in(h):
        for copy in load(h):
            copy.wait()

        def row_src(dst):
            return xs.at[h, :, pl.ds(dst * K, K)]

        row_dst = ab.at[h, :, pl.ds(0, K), pl.ds(pl.multiple_of(me_c * COLS, COLS), COLS)]

        @pl.loop(1, NC)
        def _(d):
            dst = row_peer(d)
            pltpu.make_async_remote_copy(
                src_ref=row_src(dst), dst_ref=row_dst, send_sem=in_send.at[0], recv_sem=in_recv.at[h, 0],
                device_id=(me_r, dst), device_id_type=MESH,
            ).start()

        pltpu.make_async_copy(row_src(me_c), row_dst, in_recv.at[h, 0]).start()

        @pl.loop(0, 4)
        def _(a):
            for cb in range(COLS // 16):
                for rb in range(ROWS // 16):
                    block = xs[h, a, rb * 16:rb * 16 + 16, cb * 16:cb * 16 + 16, :]
                    moved = dot_nn(perm[...], block.reshape(HALF, E)).astype(BF16)
                    xt[h, a, cb * 16:cb * 16 + 16, rb * 16:rb * 16 + 16, :] = moved.reshape(16, 16, E)

        def col_src(dst):
            return xt.at[h, :, pl.ds(dst * K, K)]

        col_dst = ab.at[h, :, pl.ds(K, K), pl.ds(pl.multiple_of(me_r * ROWS, ROWS), ROWS)]

        @pl.loop(1, NR)
        def _(d):
            dst = col_peer(d)
            pltpu.make_async_remote_copy(
                src_ref=col_src(dst), dst_ref=col_dst, send_sem=in_send.at[1], recv_sem=in_recv.at[h, 1],
                device_id=(dst, me_c), device_id_type=MESH,
            ).start()

        pltpu.make_async_copy(col_src(me_r), col_dst, in_recv.at[h, 1]).start()

    def forward(h):
        lane = lax.broadcasted_iota(jnp.int32, (HALF, E), 1)
        q_pos = lax.broadcasted_iota(jnp.int32, (HALF, HALF), 0)
        k_pos = lax.broadcasted_iota(jnp.int32, (HALF, HALF), 1)

        for part in range(2):
            here = ab.at[h, :, pl.ds(part * K, K)]
            pltpu.make_async_copy(here, here, in_recv.at[h, part]).wait()

            @pl.loop(0, K)
            def _(k):
                i = part * K + k
                allowed = k_pos <= q_pos - part
                for qb in range(2):
                    rows = pl.ds(qb * HALF, HALF)
                    query = ab[h, 0, i, rows, :]
                    scores = [
                        dot_nt(query, ab[h, 1, i, pl.ds(kb * HALF, HALF), :]) * (SCALE * LOG2E)
                        for kb in range(qb + 1)
                    ]
                    scores[qb] = jnp.where(allowed, scores[qb], NEG)
                    top = scores[0].max(axis=-1, keepdims=True)
                    for s in scores[1:]:
                        top = jnp.maximum(top, s.max(axis=-1, keepdims=True))
                    top = jnp.maximum(top, 0.1 * NEG)
                    weights = [jnp.exp2(s - top) for s in scores]
                    total = weights[0].sum(axis=-1, keepdims=True)
                    for w in weights[1:]:
                        total = total + w.sum(axis=-1, keepdims=True)
                    total = jnp.maximum(total, 1.0)
                    numer = dot_nn(weights[0].astype(BF16), ab[h, 2, i, pl.ds(0, HALF), :])
                    if qb:
                        numer = numer + dot_nn(weights[1].astype(BF16), ab[h, 2, i, pl.ds(HALF, HALF), :])
                    out = (numer / total).astype(BF16).astype(F32)
                    product = (ab[h, 3, i, rows, :].astype(F32) * out).sum(axis=-1, keepdims=True)
                    log_part = top + jnp.log2(total)
                    base = part * 8 + k
                    st[rows, :] = jnp.where(
                        lane == base, log_part, jnp.where(lane == base + 4, product, st[rows, :])
                    )

        for b in range(4):
            block = st[b * E:(b + 1) * E, :].T
            so[h, :, b * E:(b + 1) * E] = block[:16, :]

        def row_stat(dst):
            return so.at[h, pl.ds(0, 8), pl.ds(pl.multiple_of((dst // 2) * E, E), E)]

        def col_stat(dst):
            return so.at[h, pl.ds(8, 8), pl.ds(pl.multiple_of((dst // 4) * E, E), E)]

        @pl.loop(1, NC)
        def _(d):
            dst = row_peer(d)
            pltpu.make_async_remote_copy(
                src_ref=row_stat(dst), dst_ref=rs.at[h, me_c], send_sem=stat_send.at[0],
                recv_sem=stat_recv.at[h, 0], device_id=(me_r, dst), device_id_type=MESH,
            ).start()

        pltpu.make_async_copy(row_stat(me_c), rs.at[h, me_c], stat_recv.at[h, 0]).start()

        @pl.loop(1, NR)
        def _(d):
            dst = col_peer(d)
            pltpu.make_async_remote_copy(
                src_ref=col_stat(dst), dst_ref=cs.at[h, me_r], send_sem=stat_send.at[1],
                recv_sem=stat_recv.at[h, 1], device_id=(dst, me_c), device_id_type=MESH,
            ).start()

        pltpu.make_async_copy(col_stat(me_r), cs.at[h, me_r], stat_recv.at[h, 1]).start()

    def merge(h):
        pltpu.make_async_copy(rs.at[h], rs.at[h], stat_recv.at[h, 0]).wait()
        pltpu.make_async_copy(cs.at[h], cs.at[h], stat_recv.at[h, 1]).wait()
        row_values = []
        col_values = []
        for s in range(2):
            for d in range(NC):
                pr[s, 4 * d:4 * d + 4, :] = rs[h, d, 4 * s:4 * s + 4, :]
            for j in range(NR):
                pc[s, 4 * j:4 * j + 4, :] = cs[h, j, 4 * s:4 * s + 4, :]
                pc[s, COLS + 4 * j:COLS + 4 * j + 4, :] = cs[h, j, 4 * s:4 * s + 4, :]
            ct[s] = pc[s].T
            row_values.append(pr[s])
            col_values.append(ct[s, pl.ds(pl.multiple_of(me_z * ROWS, ROWS), ROWS), :])
        top = jnp.maximum(row_values[0], col_values[0])
        log_total = top + jnp.log2(jnp.exp2(row_values[0] - top) + jnp.exp2(col_values[0] - top))
        delta = (
            jnp.exp2(row_values[0] - log_total) * row_values[1]
            + jnp.exp2(col_values[0] - log_total) * col_values[1]
        )
        for s, value in enumerate((log_total, delta)):
            pr[s] = value
            lt[s, pl.ds(pl.multiple_of(me_z * ROWS, ROWS), ROWS), :] = value
            turned = lt[s].T
            pc[s, :COLS, :] = jnp.where(core == 0, turned[:COLS], turned[COLS:])
            for d in range(NC):
                mr[h, d, 4 * s:4 * s + 4, :] = pr[s, 4 * d:4 * d + 4, :]
            for j in range(NR):
                mc[h, j, 4 * s:4 * s + 4, :] = pc[s, 4 * j:4 * j + 4, :]

        @pl.loop(1, NC)
        def _(d):
            dst = row_peer(d)
            pltpu.make_async_remote_copy(
                src_ref=mr.at[h, dst], dst_ref=rr.at[h, me_c], send_sem=merged_send.at[0],
                recv_sem=merged_recv.at[h, 0], device_id=(me_r, dst), device_id_type=MESH,
            ).start()

        pltpu.make_async_copy(mr.at[h, me_c], rr.at[h, me_c], merged_recv.at[h, 0]).start()

        @pl.loop(1, NR)
        def _(d):
            dst = col_peer(d)
            pltpu.make_async_remote_copy(
                src_ref=mc.at[h, dst], dst_ref=cr.at[h, me_r], send_sem=merged_send.at[1],
                recv_sem=merged_recv.at[h, 1], device_id=(dst, me_c), device_id_type=MESH,
            ).start()

        pltpu.make_async_copy(mc.at[h, me_r], cr.at[h, me_r], merged_recv.at[h, 1]).start()

    def backward(h):
        pltpu.make_async_copy(rr.at[h], rr.at[h], merged_recv.at[h, 0]).wait()
        pltpu.make_async_copy(cr.at[h], cr.at[h], merged_recv.at[h, 1]).wait()
        lane = lax.broadcasted_iota(jnp.int32, (8, E), 1)
        for y in range(4):
            mm[0:8, y * E:(y + 1) * E] = jnp.where(lane < COLS, rr[h, 2 * y], rr[h, 2 * y + 1])
            tile = cr[h, 4 * y]
            for z in range(1, 4):
                tile = jnp.where(lane >= z * ROWS, cr[h, 4 * y + z], tile)
            mm[8:16, y * E:(y + 1) * E] = tile

        k_pos = lax.broadcasted_iota(jnp.int32, (HALF, HALF), 0)
        q_pos = lax.broadcasted_iota(jnp.int32, (HALF, HALF), 1)

        for part in range(2):

            @pl.loop(0, K)
            def _(k):
                i = part * K + k
                allowed = k_pos <= q_pos - part
                key_grads = [None, None]
                value_grads = [None, None]
                for qb in range(2):
                    rows = pl.ds(qb * HALF, HALF)
                    query = ab[h, 0, i, rows, :]
                    grad = ab[h, 3, i, rows, :]
                    log_total = mm[pl.ds(part * 8 + k, 1), rows]
                    delta = mm[pl.ds(part * 8 + 4 + k, 1), rows]
                    query_grad = None
                    out = None
                    for kb in range(qb + 1):
                        keys = ab[h, 1, i, pl.ds(kb * HALF, HALF), :]
                        values = ab[h, 2, i, pl.ds(kb * HALF, HALF), :]
                        scores = dot_nt(keys, query) * (SCALE * LOG2E)
                        if kb == qb:
                            scores = jnp.where(allowed, scores, NEG)
                        probs = jnp.exp2(scores - log_total)
                        score_grad = probs * (dot_nt(values, grad) - delta)
                        probs_half = probs.astype(BF16)
                        score_half = score_grad.astype(BF16)
                        terms = (
                            dot_nn(score_half, query), dot_nn(probs_half, grad),
                            dot_tn(keys, score_half), dot_tn(values, probs_half),
                        )
                        if kb < qb:
                            key_grads[kb] = key_grads[kb] + terms[0]
                            value_grads[kb] = value_grads[kb] + terms[1]
                        else:
                            key_grads[kb] = terms[0]
                            value_grads[kb] = terms[1]
                        query_grad = terms[2] if query_grad is None else query_grad + terms[2]
                        out = terms[3] if out is None else out + terms[3]
                    ab[h, 0, i, rows, :] = (query_grad * SCALE).T.astype(BF16)
                    ab[h, 3, i, rows, :] = out.T.astype(BF16)
                for kb in range(2):
                    where = pl.ds(kb * HALF, HALF)
                    ab[h, 1, i, where, :] = (key_grads[kb] * SCALE).astype(BF16)
                    ab[h, 2, i, where, :] = value_grads[kb].astype(BF16)

            if part == 0:

                def row_src(dst):
                    return ab.at[h, :, pl.ds(0, K), pl.ds(pl.multiple_of(dst * COLS, COLS), COLS)]

                row_dst = row_back.at[h, :, pl.ds(me_c * K, K)]

                @pl.loop(1, NC)
                def _(d):
                    dst = row_peer(d)
                    pltpu.make_async_remote_copy(
                        src_ref=row_src(dst), dst_ref=row_dst, send_sem=out_send.at[0], recv_sem=out_recv.at[0],
                        device_id=(me_r, dst), device_id_type=MESH,
                    ).start()

                pltpu.make_async_copy(row_src(me_c), row_dst, out_recv.at[0]).start()
            else:

                def col_src(dst):
                    return ab.at[h, :, pl.ds(K, K), pl.ds(pl.multiple_of(dst * ROWS, ROWS), ROWS)]

                col_dst = col_back.at[h, :, pl.ds(me_r * K, K)]

                @pl.loop(1, NR)
                def _(d):
                    dst = col_peer(d)
                    pltpu.make_async_remote_copy(
                        src_ref=col_src(dst), dst_ref=col_dst, send_sem=out_send.at[1], recv_sem=out_recv.at[1],
                        device_id=(dst, me_c), device_id_type=MESH,
                    ).start()

                pltpu.make_async_copy(col_src(me_r), col_dst, out_recv.at[1]).start()

    send_in(0)
    send_in(1)

    @pl.loop(0, H + 2)
    def _(t):
        @pl.when(t < H)
        def _():
            forward(t)

        @pl.when(t < H - 2)
        def _():
            send_in(t + 2)

        @pl.when(jnp.logical_and(t >= 1, t <= H))
        def _():
            merge(t - 1)

        @pl.when(t >= 2)
        def _():
            backward(t - 2)

    def drain(ref, sem):
        pltpu.make_async_copy(ref, ref, sem).wait()

    row_sent = ab.at[:, :, pl.ds(0, K), pl.ds(0, G - COLS)]
    col_sent = ab.at[:, :, pl.ds(0, K), pl.ds(0, G - ROWS)]
    drain(row_sent, in_send.at[0])
    drain(col_sent, in_send.at[1])
    drain(row_sent, out_send.at[0])
    drain(col_sent, out_send.at[1])
    drain(rs.at[:, pl.ds(0, NC - 1)], stat_send.at[0])
    drain(cs.at[:, pl.ds(0, NR - 1)], stat_send.at[1])
    drain(rr.at[:, pl.ds(0, NC - 1)], merged_send.at[0])
    drain(cr.at[:, pl.ds(0, NR - 1)], merged_send.at[1])
    drain(row_back, out_recv.at[0])
    drain(col_back, out_recv.at[1])


def add_kernel(row_back, col_back, q_out, k_out, v_out, o_out):
    swap = swap_matrix()
    outs = (q_out, k_out, v_out, o_out)
    for a in range(4):
        for h in range(H):
            first = row_back[h, a].reshape(HALF, E).astype(F32)
            second = dot_nn(swap, col_back[h, a].reshape(HALF, E))
            outs[a][:, :, h * E:(h + 1) * E] = (first + second).astype(BF16).reshape(16, 16, E)


def shards(query_tiles, key_tiles, value_tiles, out_grad):
    any_spec = pl.BlockSpec(memory_space=pl.ANY)
    row_back, col_back = pl.pallas_call(
        kernel,
        out_shape=(
            jax.ShapeDtypeStruct((H, 4, ROWS, COLS, E), BF16),
            jax.ShapeDtypeStruct((H, 4, COLS, ROWS, E), BF16),
        ),
        in_specs=[any_spec] * 4,
        out_specs=(any_spec, any_spec),
        scratch_shapes=[
            pltpu.VMEM((H, 4, ROWS, COLS, E), BF16),
            pltpu.VMEM((H, 4, COLS, ROWS, E), BF16),
            pltpu.VMEM((H, 4, 2 * K, G, E), BF16),
            pltpu.VMEM((HALF, HALF), BF16),
            pltpu.VMEM((G, E), F32),
            pltpu.VMEM((H, 16, G), F32),
            pltpu.VMEM((H, NC, 8, E), F32),
            pltpu.VMEM((H, NR, 8, E), F32),
            pltpu.VMEM((H, NC, 8, E), F32),
            pltpu.VMEM((H, NR, 8, E), F32),
            pltpu.VMEM((H, NC, 8, E), F32),
            pltpu.VMEM((H, NR, 8, E), F32),
            pltpu.VMEM((16, G), F32),
            pltpu.VMEM((2, ROWS, E), F32),
            pltpu.VMEM((2, E, E), F32),
            pltpu.VMEM((2, E, E), F32),
            pltpu.VMEM((2, E, E), F32),
            pltpu.SemaphoreType.DMA((H, 4)),
            pltpu.SemaphoreType.DMA((2,)),
            pltpu.SemaphoreType.DMA((H, 2)),
            pltpu.SemaphoreType.DMA((2,)),
            pltpu.SemaphoreType.DMA((2,)),
            pltpu.SemaphoreType.DMA((2,)),
            pltpu.SemaphoreType.DMA((H, 2)),
            pltpu.SemaphoreType.DMA((2,)),
            pltpu.SemaphoreType.DMA((H, 2)),
        ],
        compiler_params=pltpu.CompilerParams(
            collective_id=0, has_side_effects=True, vmem_limit_bytes=52 * 2**20
        ),
        name="attend",
    )(query_tiles, key_tiles, value_tiles, out_grad)
    out = jax.ShapeDtypeStruct((ROWS, COLS, H * E), BF16)
    query_grad, key_grad, value_grad, attended = pl.pallas_call(
        add_kernel,
        out_shape=(out,) * 4,
        grid=(ROWS // 16, COLS // 16),
        in_specs=[
            pl.BlockSpec((H, 4, 16, 16, E), lambda r, c: (0, 0, r, c, 0)),
            pl.BlockSpec((H, 4, 16, 16, E), lambda r, c: (0, 0, c, r, 0)),
        ],
        out_specs=[pl.BlockSpec((16, 16, H * E), lambda r, c: (r, c, 0))] * 4,
        compiler_params=pltpu.CompilerParams(vmem_limit_bytes=32 * 2**20),
        name="add_parts",
    )(row_back, col_back)
    return attended, query_grad, key_grad, value_grad


def solution(mesh):
    spec = P("row", "col", None)
    return jax.shard_map(
        shards, mesh=mesh, in_specs=(spec,) * 4, out_specs=(spec,) * 4, check_vma=False
    )
```

```python
import functools

import jax
import jax.numpy as jnp
from jax import lax
from jax.experimental import pallas as pl
from jax.experimental.pallas import tpu as pltpu
from jax.sharding import PartitionSpec as P

H = 4
E = 128
G = 512
ROWS = 32
COLS = 64
NR = 16
NC = 8
K = 4
HALF = 256
LOG2E = 1.4426950408889634
SCALE = E ** (-0.5)
NEG = -1e30
MESH = pl.DeviceIdType.MESH
F32 = jnp.float32
BF16 = jnp.bfloat16


def dot_nn(a, b):
    return lax.dot_general(a, b, (((1,), (0,)), ((), ())), preferred_element_type=F32)


def dot_nt(a, b):
    return lax.dot_general(a, b, (((1,), (1,)), ((), ())), preferred_element_type=F32)


def dot_tn(a, b):
    return lax.dot_general(a, b, (((0,), (0,)), ((), ())), preferred_element_type=F32)


def swap_matrix():
    to = lax.broadcasted_iota(jnp.int32, (HALF, HALF), 0)
    of = lax.broadcasted_iota(jnp.int32, (HALF, HALF), 1)
    match = of == (to % 16) * 16 + to // 16
    return jnp.where(match, 1.0, 0.0).astype(BF16)


def kernel(
    q_in, k_in, v_in, g_in, row_back, col_back,
    xs, xt, ab, perm, st, so, rs, cs, mr, mc, rr, cr, mm, pr, pc, ct, lt,
    load_sem, in_send, in_recv, out_send, out_recv, stat_send, stat_recv, merged_send, merged_recv,
):
    me_r = lax.axis_index("row")
    me_c = lax.axis_index("col")
    core = lax.rem(me_c, 2)
    me_z = lax.rem(me_r, 4)
    inputs = (q_in, k_in, v_in, g_in)

    def row_peer(d):
        return lax.rem(me_c + d, NC)

    def col_peer(d):
        return lax.rem(me_r + d, NR)

    def load(h):
        return [
            pltpu.make_async_copy(
                inputs[a].at[:, :, pl.ds(pl.multiple_of(h * E, E), E)], xs.at[h, a], load_sem.at[h, a]
            )
            for a in range(4)
        ]

    for h in range(H):
        for copy in load(h):
            copy.start()

    barrier = pltpu.get_barrier_semaphore()

    @pl.loop(1, NC)
    def _(d):
        pl.semaphore_signal(barrier, inc=1, device_id=(me_r, row_peer(d)), device_id_type=MESH)

    @pl.loop(1, NR)
    def _(d):
        pl.semaphore_signal(barrier, inc=1, device_id=(col_peer(d), me_c), device_id_type=MESH)

    perm[...] = swap_matrix()
    st[...] = jnp.zeros_like(st)
    lt[...] = jnp.zeros_like(lt)
    pl.semaphore_wait(barrier, NC + NR - 2)

    def send_in(h):
        for copy in load(h):
            copy.wait()

        def row_src(dst):
            return xs.at[h, :, pl.ds(dst * K, K)]

        row_dst = ab.at[h, :, pl.ds(0, K), pl.ds(pl.multiple_of(me_c * COLS, COLS), COLS)]

        @pl.loop(1, NC)
        def _(d):
            dst = row_peer(d)
            pltpu.make_async_remote_copy(
                src_ref=row_src(dst), dst_ref=row_dst, send_sem=in_send.at[0], recv_sem=in_recv.at[h, 0],
                device_id=(me_r, dst), device_id_type=MESH,
            ).start()

        pltpu.make_async_copy(row_src(me_c), row_dst, in_recv.at[h, 0]).start()

        @pl.loop(0, 4)
        def _(a):
            for cb in range(COLS // 16):
                for rb in range(ROWS // 16):
                    block = xs[h, a, rb * 16:rb * 16 + 16, cb * 16:cb * 16 + 16, :]
                    moved = dot_nn(perm[...], block.reshape(HALF, E)).astype(BF16)
                    xt[h, a, cb * 16:cb * 16 + 16, rb * 16:rb * 16 + 16, :] = moved.reshape(16, 16, E)

            def col_src(dst):
                return xt.at[h, a, pl.ds(dst * K, K)]

            col_dst = ab.at[h, a, pl.ds(K, K), pl.ds(pl.multiple_of(me_r * ROWS, ROWS), ROWS)]

            @pl.loop(1, NR)
            def _(d):
                dst = col_peer(d)
                pltpu.make_async_remote_copy(
                    src_ref=col_src(dst), dst_ref=col_dst, send_sem=in_send.at[1], recv_sem=in_recv.at[h, 1],
                    device_id=(dst, me_c), device_id_type=MESH,
                ).start()

            pltpu.make_async_copy(col_src(me_r), col_dst, in_recv.at[h, 1]).start()

    def forward(h):
        lane = lax.broadcasted_iota(jnp.int32, (HALF, E), 1)
        q_pos = lax.broadcasted_iota(jnp.int32, (HALF, HALF), 0)
        k_pos = lax.broadcasted_iota(jnp.int32, (HALF, HALF), 1)

        for part in range(2):
            here = ab.at[h, :, pl.ds(part * K, K)]
            pltpu.make_async_copy(here, here, in_recv.at[h, part]).wait()

            @pl.loop(0, K)
            def _(k):
                i = part * K + k
                allowed = k_pos <= q_pos - part
                for qb in range(2):
                    rows = pl.ds(qb * HALF, HALF)
                    query = ab[h, 0, i, rows, :]
                    scores = [
                        dot_nt(query, ab[h, 1, i, pl.ds(kb * HALF, HALF), :]) * (SCALE * LOG2E)
                        for kb in range(qb + 1)
                    ]
                    scores[qb] = jnp.where(allowed, scores[qb], NEG)
                    top = scores[0].max(axis=-1, keepdims=True)
                    for s in scores[1:]:
                        top = jnp.maximum(top, s.max(axis=-1, keepdims=True))
                    top = jnp.maximum(top, 0.1 * NEG)
                    weights = [jnp.exp2(s - top) for s in scores]
                    total = weights[0].sum(axis=-1, keepdims=True)
                    for w in weights[1:]:
                        total = total + w.sum(axis=-1, keepdims=True)
                    total = jnp.maximum(total, 1.0)
                    numer = dot_nn(weights[0].astype(BF16), ab[h, 2, i, pl.ds(0, HALF), :])
                    if qb:
                        numer = numer + dot_nn(weights[1].astype(BF16), ab[h, 2, i, pl.ds(HALF, HALF), :])
                    out = (numer / total).astype(BF16).astype(F32)
                    product = (ab[h, 3, i, rows, :].astype(F32) * out).sum(axis=-1, keepdims=True)
                    log_part = top + jnp.log2(total)
                    base = part * 8 + k
                    st[rows, :] = jnp.where(
                        lane == base, log_part, jnp.where(lane == base + 4, product, st[rows, :])
                    )

        for b in range(4):
            block = st[b * E:(b + 1) * E, :].T
            so[h, :, b * E:(b + 1) * E] = block[:16, :]

        def row_stat(dst):
            return so.at[h, pl.ds(0, 8), pl.ds(pl.multiple_of((dst // 2) * E, E), E)]

        def col_stat(dst):
            return so.at[h, pl.ds(8, 8), pl.ds(pl.multiple_of((dst // 4) * E, E), E)]

        @pl.loop(1, NC)
        def _(d):
            dst = row_peer(d)
            pltpu.make_async_remote_copy(
                src_ref=row_stat(dst), dst_ref=rs.at[h, me_c], send_sem=stat_send.at[0],
                recv_sem=stat_recv.at[h, 0], device_id=(me_r, dst), device_id_type=MESH,
            ).start()

        pltpu.make_async_copy(row_stat(me_c), rs.at[h, me_c], stat_recv.at[h, 0]).start()

        @pl.loop(1, NR)
        def _(d):
            dst = col_peer(d)
            pltpu.make_async_remote_copy(
                src_ref=col_stat(dst), dst_ref=cs.at[h, me_r], send_sem=stat_send.at[1],
                recv_sem=stat_recv.at[h, 1], device_id=(dst, me_c), device_id_type=MESH,
            ).start()

        pltpu.make_async_copy(col_stat(me_r), cs.at[h, me_r], stat_recv.at[h, 1]).start()

    def merge(h):
        pltpu.make_async_copy(rs.at[h], rs.at[h], stat_recv.at[h, 0]).wait()
        pltpu.make_async_copy(cs.at[h], cs.at[h], stat_recv.at[h, 1]).wait()
        row_values = []
        col_values = []
        for s in range(2):
            for d in range(NC):
                pr[s, 4 * d:4 * d + 4, :] = rs[h, d, 4 * s:4 * s + 4, :]
            for j in range(NR):
                pc[s, 4 * j:4 * j + 4, :] = cs[h, j, 4 * s:4 * s + 4, :]
                pc[s, COLS + 4 * j:COLS + 4 * j + 4, :] = cs[h, j, 4 * s:4 * s + 4, :]
            ct[s] = pc[s].T
            row_values.append(pr[s])
            col_values.append(ct[s, pl.ds(pl.multiple_of(me_z * ROWS, ROWS), ROWS), :])
        top = jnp.maximum(row_values[0], col_values[0])
        log_total = top + jnp.log2(jnp.exp2(row_values[0] - top) + jnp.exp2(col_values[0] - top))
        delta = (
            jnp.exp2(row_values[0] - log_total) * row_values[1]
            + jnp.exp2(col_values[0] - log_total) * col_values[1]
        )
        for s, value in enumerate((log_total, delta)):
            pr[s] = value
            lt[s, pl.ds(pl.multiple_of(me_z * ROWS, ROWS), ROWS), :] = value
            turned = lt[s].T
            pc[s, :COLS, :] = jnp.where(core == 0, turned[:COLS], turned[COLS:])
            for d in range(NC):
                mr[h, d, 4 * s:4 * s + 4, :] = pr[s, 4 * d:4 * d + 4, :]
            for j in range(NR):
                mc[h, j, 4 * s:4 * s + 4, :] = pc[s, 4 * j:4 * j + 4, :]

        @pl.loop(1, NC)
        def _(d):
            dst = row_peer(d)
            pltpu.make_async_remote_copy(
                src_ref=mr.at[h, dst], dst_ref=rr.at[h, me_c], send_sem=merged_send.at[0],
                recv_sem=merged_recv.at[h, 0], device_id=(me_r, dst), device_id_type=MESH,
            ).start()

        pltpu.make_async_copy(mr.at[h, me_c], rr.at[h, me_c], merged_recv.at[h, 0]).start()

        @pl.loop(1, NR)
        def _(d):
            dst = col_peer(d)
            pltpu.make_async_remote_copy(
                src_ref=mc.at[h, dst], dst_ref=cr.at[h, me_r], send_sem=merged_send.at[1],
                recv_sem=merged_recv.at[h, 1], device_id=(dst, me_c), device_id_type=MESH,
            ).start()

        pltpu.make_async_copy(mc.at[h, me_r], cr.at[h, me_r], merged_recv.at[h, 1]).start()

    def backward(h):
        pltpu.make_async_copy(rr.at[h], rr.at[h], merged_recv.at[h, 0]).wait()
        pltpu.make_async_copy(cr.at[h], cr.at[h], merged_recv.at[h, 1]).wait()
        lane = lax.broadcasted_iota(jnp.int32, (8, E), 1)
        for y in range(4):
            mm[0:8, y * E:(y + 1) * E] = jnp.where(lane < COLS, rr[h, 2 * y], rr[h, 2 * y + 1])
            tile = cr[h, 4 * y]
            for z in range(1, 4):
                tile = jnp.where(lane >= z * ROWS, cr[h, 4 * y + z], tile)
            mm[8:16, y * E:(y + 1) * E] = tile

        k_pos = lax.broadcasted_iota(jnp.int32, (HALF, HALF), 0)
        q_pos = lax.broadcasted_iota(jnp.int32, (HALF, HALF), 1)

        for part in range(2):

            @pl.loop(0, K)
            def _(k):
                i = part * K + k
                allowed = k_pos <= q_pos - part
                key_grads = [None, None]
                value_grads = [None, None]
                for qb in range(2):
                    rows = pl.ds(qb * HALF, HALF)
                    query = ab[h, 0, i, rows, :]
                    grad = ab[h, 3, i, rows, :]
                    log_total = mm[pl.ds(part * 8 + k, 1), rows]
                    delta = mm[pl.ds(part * 8 + 4 + k, 1), rows]
                    query_grad = None
                    out = None
                    for kb in range(qb + 1):
                        keys = ab[h, 1, i, pl.ds(kb * HALF, HALF), :]
                        values = ab[h, 2, i, pl.ds(kb * HALF, HALF), :]
                        scores = dot_nt(keys, query) * (SCALE * LOG2E)
                        if kb == qb:
                            scores = jnp.where(allowed, scores, NEG)
                        probs = jnp.exp2(scores - log_total)
                        score_grad = probs * (dot_nt(values, grad) - delta)
                        probs_half = probs.astype(BF16)
                        score_half = score_grad.astype(BF16)
                        terms = (
                            dot_nn(score_half, query), dot_nn(probs_half, grad),
                            dot_tn(keys, score_half), dot_tn(values, probs_half),
                        )
                        if kb < qb:
                            key_grads[kb] = key_grads[kb] + terms[0]
                            value_grads[kb] = value_grads[kb] + terms[1]
                        else:
                            key_grads[kb] = terms[0]
                            value_grads[kb] = terms[1]
                        query_grad = terms[2] if query_grad is None else query_grad + terms[2]
                        out = terms[3] if out is None else out + terms[3]
                    ab[h, 0, i, rows, :] = (query_grad * SCALE).T.astype(BF16)
                    ab[h, 3, i, rows, :] = out.T.astype(BF16)
                for kb in range(2):
                    where = pl.ds(kb * HALF, HALF)
                    ab[h, 1, i, where, :] = (key_grads[kb] * SCALE).astype(BF16)
                    ab[h, 2, i, where, :] = value_grads[kb].astype(BF16)

            if part == 0:

                def row_src(dst):
                    return ab.at[h, :, pl.ds(0, K), pl.ds(pl.multiple_of(dst * COLS, COLS), COLS)]

                row_dst = row_back.at[h, :, pl.ds(me_c * K, K)]

                @pl.loop(1, NC)
                def _(d):
                    dst = row_peer(d)
                    pltpu.make_async_remote_copy(
                        src_ref=row_src(dst), dst_ref=row_dst, send_sem=out_send.at[0], recv_sem=out_recv.at[0],
                        device_id=(me_r, dst), device_id_type=MESH,
                    ).start()

                pltpu.make_async_copy(row_src(me_c), row_dst, out_recv.at[0]).start()
            else:

                @pl.loop(0, 4)
                def _(a):
                    def col_src(dst):
                        return ab.at[h, a, pl.ds(K, K), pl.ds(pl.multiple_of(dst * ROWS, ROWS), ROWS)]

                    col_dst = col_back.at[h, a, pl.ds(me_r * K, K)]

                    @pl.loop(1, NR)
                    def _(d):
                        dst = col_peer(d)
                        pltpu.make_async_remote_copy(
                            src_ref=col_src(dst), dst_ref=col_dst, send_sem=out_send.at[1],
                            recv_sem=out_recv.at[1], device_id=(dst, me_c), device_id_type=MESH,
                        ).start()

                    pltpu.make_async_copy(col_src(me_r), col_dst, out_recv.at[1]).start()

    send_in(0)
    send_in(1)

    @pl.loop(0, H + 2)
    def _(t):
        @pl.when(t < H)
        def _():
            forward(t)

        @pl.when(t < H - 2)
        def _():
            send_in(t + 2)

        @pl.when(jnp.logical_and(t >= 1, t <= H))
        def _():
            merge(t - 1)

        @pl.when(t >= 2)
        def _():
            backward(t - 2)

    def drain(ref, sem):
        pltpu.make_async_copy(ref, ref, sem).wait()

    row_sent = ab.at[:, :, pl.ds(0, K), pl.ds(0, G - COLS)]
    col_sent = ab.at[:, :, pl.ds(0, K), pl.ds(0, G - ROWS)]
    drain(row_sent, in_send.at[0])
    drain(col_sent, in_send.at[1])
    drain(row_sent, out_send.at[0])
    drain(col_sent, out_send.at[1])
    drain(rs.at[:, pl.ds(0, NC - 1)], stat_send.at[0])
    drain(cs.at[:, pl.ds(0, NR - 1)], stat_send.at[1])
    drain(rr.at[:, pl.ds(0, NC - 1)], merged_send.at[0])
    drain(cr.at[:, pl.ds(0, NR - 1)], merged_send.at[1])
    drain(row_back, out_recv.at[0])
    drain(col_back, out_recv.at[1])


def add_kernel(row_back, col_back, q_out, k_out, v_out, o_out):
    swap = swap_matrix()
    outs = (q_out, k_out, v_out, o_out)
    for a in range(4):
        for h in range(H):
            first = row_back[h, a].reshape(HALF, E).astype(F32)
            second = dot_nn(swap, col_back[h, a].reshape(HALF, E))
            outs[a][:, :, h * E:(h + 1) * E] = (first + second).astype(BF16).reshape(16, 16, E)


def shards(query_tiles, key_tiles, value_tiles, out_grad):
    any_spec = pl.BlockSpec(memory_space=pl.ANY)
    row_back, col_back = pl.pallas_call(
        kernel,
        out_shape=(
            jax.ShapeDtypeStruct((H, 4, ROWS, COLS, E), BF16),
            jax.ShapeDtypeStruct((H, 4, COLS, ROWS, E), BF16),
        ),
        in_specs=[any_spec] * 4,
        out_specs=(any_spec, any_spec),
        scratch_shapes=[
            pltpu.VMEM((H, 4, ROWS, COLS, E), BF16),
            pltpu.VMEM((H, 4, COLS, ROWS, E), BF16),
            pltpu.VMEM((H, 4, 2 * K, G, E), BF16),
            pltpu.VMEM((HALF, HALF), BF16),
            pltpu.VMEM((G, E), F32),
            pltpu.VMEM((H, 16, G), F32),
            pltpu.VMEM((H, NC, 8, E), F32),
            pltpu.VMEM((H, NR, 8, E), F32),
            pltpu.VMEM((H, NC, 8, E), F32),
            pltpu.VMEM((H, NR, 8, E), F32),
            pltpu.VMEM((H, NC, 8, E), F32),
            pltpu.VMEM((H, NR, 8, E), F32),
            pltpu.VMEM((16, G), F32),
            pltpu.VMEM((2, ROWS, E), F32),
            pltpu.VMEM((2, E, E), F32),
            pltpu.VMEM((2, E, E), F32),
            pltpu.VMEM((2, E, E), F32),
            pltpu.SemaphoreType.DMA((H, 4)),
            pltpu.SemaphoreType.DMA((2,)),
            pltpu.SemaphoreType.DMA((H, 2)),
            pltpu.SemaphoreType.DMA((2,)),
            pltpu.SemaphoreType.DMA((2,)),
            pltpu.SemaphoreType.DMA((2,)),
            pltpu.SemaphoreType.DMA((H, 2)),
            pltpu.SemaphoreType.DMA((2,)),
            pltpu.SemaphoreType.DMA((H, 2)),
        ],
        compiler_params=pltpu.CompilerParams(
            collective_id=0, has_side_effects=True, vmem_limit_bytes=52 * 2**20
        ),
        name="attend",
    )(query_tiles, key_tiles, value_tiles, out_grad)
    out = jax.ShapeDtypeStruct((ROWS, COLS, H * E), BF16)
    query_grad, key_grad, value_grad, attended = pl.pallas_call(
        add_kernel,
        out_shape=(out,) * 4,
        grid=(ROWS // 16, COLS // 16),
        in_specs=[
            pl.BlockSpec((H, 4, 16, 16, E), lambda r, c: (0, 0, r, c, 0)),
            pl.BlockSpec((H, 4, 16, 16, E), lambda r, c: (0, 0, c, r, 0)),
        ],
        out_specs=[pl.BlockSpec((16, 16, H * E), lambda r, c: (r, c, 0))] * 4,
        compiler_params=pltpu.CompilerParams(vmem_limit_bytes=60 * 2**20),
        name="add_parts",
    )(row_back, col_back)
    return attended, query_grad, key_grad, value_grad


def solution(mesh):
    spec = P("row", "col", None)
    return jax.shard_map(
        shards, mesh=mesh, in_specs=(spec,) * 4, out_specs=(spec,) * 4, check_vma=False
    )
```

```python
import functools

import jax
import jax.numpy as jnp
from jax import lax
from jax.experimental import pallas as pl
from jax.experimental.pallas import tpu as pltpu
from jax.sharding import PartitionSpec as P

H = 4
E = 128
G = 512
ROWS = 32
COLS = 64
NR = 16
NC = 8
K = 4
HALF = 256
LOG2E = 1.4426950408889634
SCALE = E ** (-0.5)
NEG = -1e30
MOVES = 2
MESH = pl.DeviceIdType.MESH
F32 = jnp.float32
BF16 = jnp.bfloat16


def dot_nn(a, b):
    return lax.dot_general(a, b, (((1,), (0,)), ((), ())), preferred_element_type=F32)


def dot_nt(a, b):
    return lax.dot_general(a, b, (((1,), (1,)), ((), ())), preferred_element_type=F32)


def dot_tn(a, b):
    return lax.dot_general(a, b, (((0,), (0,)), ((), ())), preferred_element_type=F32)


def swap_matrix():
    to = lax.broadcasted_iota(jnp.int32, (HALF, HALF), 0)
    of = lax.broadcasted_iota(jnp.int32, (HALF, HALF), 1)
    match = of == (to % 16) * 16 + to // 16
    return jnp.where(match, 1.0, 0.0).astype(BF16)


def kernel(
    q_in, k_in, v_in, g_in, row_back, col_back, q_sum, k_sum, v_sum, o_sum,
    xs, xt, ab, perm, st, so, rs, cs, mr, mc, rr, cr, mm, pr, pc, ct, lt,
    load_sem, in_send, in_recv, out_send, out_recv, stat_send, stat_recv, merged_send, merged_recv,
    back_sem, sum_sem,
):
    me_r = lax.axis_index("row")
    me_c = lax.axis_index("col")
    core = lax.rem(me_c, 2)
    me_z = lax.rem(me_r, 4)
    inputs = (q_in, k_in, v_in, g_in)

    def row_peer(d):
        return lax.rem(me_c + d, NC)

    def col_peer(d):
        return lax.rem(me_r + d, NR)

    def load(h):
        return [
            pltpu.make_async_copy(
                inputs[a].at[:, :, pl.ds(pl.multiple_of(h * E, E), E)], xs.at[h, a], load_sem.at[h, a]
            )
            for a in range(4)
        ]

    for copy in load(0):
        copy.start()

    barrier = pltpu.get_barrier_semaphore()

    @pl.loop(1, NC)
    def _(d):
        pl.semaphore_signal(barrier, inc=1, device_id=(me_r, row_peer(d)), device_id_type=MESH)

    @pl.loop(1, NR)
    def _(d):
        pl.semaphore_signal(barrier, inc=1, device_id=(col_peer(d), me_c), device_id_type=MESH)

    perm[...] = swap_matrix()
    st[...] = jnp.zeros_like(st)
    lt[...] = jnp.zeros_like(lt)
    pl.semaphore_wait(barrier, NC + NR - 2)

    def send_in(h):
        for copy in load(h):
            copy.wait()

        @pl.when(h < H - 1)
        def _():
            for copy in load(h + 1):
                copy.start()

        def row_src(dst):
            return xs.at[h, :, pl.ds(dst * K, K)]

        row_dst = ab.at[h, :, pl.ds(0, K), pl.ds(pl.multiple_of(me_c * COLS, COLS), COLS)]

        @pl.loop(1, NC)
        def _(d):
            dst = row_peer(d)
            pltpu.make_async_remote_copy(
                src_ref=row_src(dst), dst_ref=row_dst, send_sem=in_send.at[0], recv_sem=in_recv.at[h, 0],
                device_id=(me_r, dst), device_id_type=MESH,
            ).start()

        pltpu.make_async_copy(row_src(me_c), row_dst, in_recv.at[h, 0]).start()

        @pl.loop(0, 4)
        def _(a):
            for cb in range(COLS // 16):
                for rb in range(ROWS // 16):
                    block = xs[h, a, rb * 16:rb * 16 + 16, cb * 16:cb * 16 + 16, :]
                    moved = dot_nn(perm[...], block.reshape(HALF, E)).astype(BF16)
                    xt[h, a, cb * 16:cb * 16 + 16, rb * 16:rb * 16 + 16, :] = moved.reshape(16, 16, E)

            def col_src(dst):
                return xt.at[h, a, pl.ds(dst * K, K)]

            col_dst = ab.at[h, a, pl.ds(K, K), pl.ds(pl.multiple_of(me_r * ROWS, ROWS), ROWS)]

            @pl.loop(1, NR)
            def _(d):
                dst = col_peer(d)
                pltpu.make_async_remote_copy(
                    src_ref=col_src(dst), dst_ref=col_dst, send_sem=in_send.at[1], recv_sem=in_recv.at[h, 1],
                    device_id=(dst, me_c), device_id_type=MESH,
                ).start()

            pltpu.make_async_copy(col_src(me_r), col_dst, in_recv.at[h, 1]).start()

    def forward(h):
        lane = lax.broadcasted_iota(jnp.int32, (HALF, E), 1)
        q_pos = lax.broadcasted_iota(jnp.int32, (HALF, HALF), 0)
        k_pos = lax.broadcasted_iota(jnp.int32, (HALF, HALF), 1)

        for part in range(2):
            here = ab.at[h, :, pl.ds(part * K, K)]
            pltpu.make_async_copy(here, here, in_recv.at[h, part]).wait()

            @pl.loop(0, K)
            def _(k):
                i = part * K + k
                allowed = k_pos <= q_pos - part
                for qb in range(2):
                    rows = pl.ds(qb * HALF, HALF)
                    query = ab[h, 0, i, rows, :]
                    scores = [
                        dot_nt(query, ab[h, 1, i, pl.ds(kb * HALF, HALF), :]) * (SCALE * LOG2E)
                        for kb in range(qb + 1)
                    ]
                    scores[qb] = jnp.where(allowed, scores[qb], NEG)
                    top = scores[0].max(axis=-1, keepdims=True)
                    for s in scores[1:]:
                        top = jnp.maximum(top, s.max(axis=-1, keepdims=True))
                    top = jnp.maximum(top, 0.1 * NEG)
                    weights = [jnp.exp2(s - top) for s in scores]
                    total = weights[0].sum(axis=-1, keepdims=True)
                    for w in weights[1:]:
                        total = total + w.sum(axis=-1, keepdims=True)
                    total = jnp.maximum(total, 1.0)
                    numer = dot_nn(weights[0].astype(BF16), ab[h, 2, i, pl.ds(0, HALF), :])
                    if qb:
                        numer = numer + dot_nn(weights[1].astype(BF16), ab[h, 2, i, pl.ds(HALF, HALF), :])
                    out = (numer / total).astype(BF16).astype(F32)
                    product = (ab[h, 3, i, rows, :].astype(F32) * out).sum(axis=-1, keepdims=True)
                    log_part = top + jnp.log2(total)
                    base = part * 8 + k
                    st[rows, :] = jnp.where(
                        lane == base, log_part, jnp.where(lane == base + 4, product, st[rows, :])
                    )

        for b in range(4):
            block = st[b * E:(b + 1) * E, :].T
            so[h, :, b * E:(b + 1) * E] = block[:16, :]

        def row_stat(dst):
            return so.at[h, pl.ds(0, 8), pl.ds(pl.multiple_of((dst // 2) * E, E), E)]

        def col_stat(dst):
            return so.at[h, pl.ds(8, 8), pl.ds(pl.multiple_of((dst // 4) * E, E), E)]

        @pl.loop(1, NC)
        def _(d):
            dst = row_peer(d)
            pltpu.make_async_remote_copy(
                src_ref=row_stat(dst), dst_ref=rs.at[h, me_c], send_sem=stat_send.at[0],
                recv_sem=stat_recv.at[h, 0], device_id=(me_r, dst), device_id_type=MESH,
            ).start()

        pltpu.make_async_copy(row_stat(me_c), rs.at[h, me_c], stat_recv.at[h, 0]).start()

        @pl.loop(1, NR)
        def _(d):
            dst = col_peer(d)
            pltpu.make_async_remote_copy(
                src_ref=col_stat(dst), dst_ref=cs.at[h, me_r], send_sem=stat_send.at[1],
                recv_sem=stat_recv.at[h, 1], device_id=(dst, me_c), device_id_type=MESH,
            ).start()

        pltpu.make_async_copy(col_stat(me_r), cs.at[h, me_r], stat_recv.at[h, 1]).start()

    def merge(h):
        pltpu.make_async_copy(rs.at[h], rs.at[h], stat_recv.at[h, 0]).wait()
        pltpu.make_async_copy(cs.at[h], cs.at[h], stat_recv.at[h, 1]).wait()
        row_values = []
        col_values = []
        for s in range(2):
            for d in range(NC):
                pr[s, 4 * d:4 * d + 4, :] = rs[h, d, 4 * s:4 * s + 4, :]
            for j in range(NR):
                pc[s, 4 * j:4 * j + 4, :] = cs[h, j, 4 * s:4 * s + 4, :]
                pc[s, COLS + 4 * j:COLS + 4 * j + 4, :] = cs[h, j, 4 * s:4 * s + 4, :]
            ct[s] = pc[s].T
            row_values.append(pr[s])
            col_values.append(ct[s, pl.ds(pl.multiple_of(me_z * ROWS, ROWS), ROWS), :])
        top = jnp.maximum(row_values[0], col_values[0])
        log_total = top + jnp.log2(jnp.exp2(row_values[0] - top) + jnp.exp2(col_values[0] - top))
        delta = (
            jnp.exp2(row_values[0] - log_total) * row_values[1]
            + jnp.exp2(col_values[0] - log_total) * col_values[1]
        )
        for s, value in enumerate((log_total, delta)):
            pr[s] = value
            lt[s, pl.ds(pl.multiple_of(me_z * ROWS, ROWS), ROWS), :] = value
            turned = lt[s].T
            pc[s, :COLS, :] = jnp.where(core == 0, turned[:COLS], turned[COLS:])
            for d in range(NC):
                mr[h, d, 4 * s:4 * s + 4, :] = pr[s, 4 * d:4 * d + 4, :]
            for j in range(NR):
                mc[h, j, 4 * s:4 * s + 4, :] = pc[s, 4 * j:4 * j + 4, :]

        @pl.loop(1, NC)
        def _(d):
            dst = row_peer(d)
            pltpu.make_async_remote_copy(
                src_ref=mr.at[h, dst], dst_ref=rr.at[h, me_c], send_sem=merged_send.at[0],
                recv_sem=merged_recv.at[h, 0], device_id=(me_r, dst), device_id_type=MESH,
            ).start()

        pltpu.make_async_copy(mr.at[h, me_c], rr.at[h, me_c], merged_recv.at[h, 0]).start()

        @pl.loop(1, NR)
        def _(d):
            dst = col_peer(d)
            pltpu.make_async_remote_copy(
                src_ref=mc.at[h, dst], dst_ref=cr.at[h, me_r], send_sem=merged_send.at[1],
                recv_sem=merged_recv.at[h, 1], device_id=(dst, me_c), device_id_type=MESH,
            ).start()

        pltpu.make_async_copy(mc.at[h, me_r], cr.at[h, me_r], merged_recv.at[h, 1]).start()

    def backward(h):
        pltpu.make_async_copy(rr.at[h], rr.at[h], merged_recv.at[h, 0]).wait()
        pltpu.make_async_copy(cr.at[h], cr.at[h], merged_recv.at[h, 1]).wait()
        lane = lax.broadcasted_iota(jnp.int32, (8, E), 1)
        for y in range(4):
            mm[0:8, y * E:(y + 1) * E] = jnp.where(lane < COLS, rr[h, 2 * y], rr[h, 2 * y + 1])
            tile = cr[h, 4 * y]
            for z in range(1, 4):
                tile = jnp.where(lane >= z * ROWS, cr[h, 4 * y + z], tile)
            mm[8:16, y * E:(y + 1) * E] = tile

        k_pos = lax.broadcasted_iota(jnp.int32, (HALF, HALF), 0)
        q_pos = lax.broadcasted_iota(jnp.int32, (HALF, HALF), 1)

        def instance(part, k):
            i = part * K + k
            allowed = k_pos <= q_pos - part
            key_grads = [None, None]
            value_grads = [None, None]
            for qb in range(2):
                rows = pl.ds(qb * HALF, HALF)
                query = ab[h, 0, i, rows, :]
                grad = ab[h, 3, i, rows, :]
                log_total = mm[pl.ds(part * 8 + k, 1), rows]
                delta = mm[pl.ds(part * 8 + 4 + k, 1), rows]
                query_grad = None
                out = None
                for kb in range(qb + 1):
                    keys = ab[h, 1, i, pl.ds(kb * HALF, HALF), :]
                    values = ab[h, 2, i, pl.ds(kb * HALF, HALF), :]
                    scores = dot_nt(keys, query) * (SCALE * LOG2E)
                    if kb == qb:
                        scores = jnp.where(allowed, scores, NEG)
                    probs = jnp.exp2(scores - log_total)
                    score_grad = probs * (dot_nt(values, grad) - delta)
                    probs_half = probs.astype(BF16)
                    score_half = score_grad.astype(BF16)
                    terms = (
                        dot_nn(score_half, query), dot_nn(probs_half, grad),
                        dot_tn(keys, score_half), dot_tn(values, probs_half),
                    )
                    if kb < qb:
                        key_grads[kb] = key_grads[kb] + terms[0]
                        value_grads[kb] = value_grads[kb] + terms[1]
                    else:
                        key_grads[kb] = terms[0]
                        value_grads[kb] = terms[1]
                    query_grad = terms[2] if query_grad is None else query_grad + terms[2]
                    out = terms[3] if out is None else out + terms[3]
                ab[h, 0, i, rows, :] = (query_grad * SCALE).T.astype(BF16)
                ab[h, 3, i, rows, :] = out.T.astype(BF16)
            for kb in range(2):
                where = pl.ds(kb * HALF, HALF)
                ab[h, 1, i, where, :] = (key_grads[kb] * SCALE).astype(BF16)
                ab[h, 2, i, where, :] = value_grads[kb].astype(BF16)

        @pl.loop(0, K)
        def _(k):
            instance(0, k)

            def row_src(dst):
                return ab.at[h, :, k, pl.ds(pl.multiple_of(dst * COLS, COLS), COLS)]

            row_dst = row_back.at[h, :, me_c * K + k]

            @pl.loop(1, NC)
            def _(d):
                dst = row_peer(d)
                pltpu.make_async_remote_copy(
                    src_ref=row_src(dst), dst_ref=row_dst, send_sem=out_send.at[0],
                    recv_sem=out_recv.at[h, 0], device_id=(me_r, dst), device_id_type=MESH,
                ).start()

            pltpu.make_async_copy(row_src(me_c), row_dst, out_recv.at[h, 0]).start()
            instance(1, k)

            def col_src(dst):
                return ab.at[h, :, K + k, pl.ds(pl.multiple_of(dst * ROWS, ROWS), ROWS)]

            col_dst = col_back.at[h, :, me_r * K + k]

            @pl.loop(1, NR)
            def _(d):
                dst = col_peer(d)
                pltpu.make_async_remote_copy(
                    src_ref=col_src(dst), dst_ref=col_dst, send_sem=out_send.at[1],
                    recv_sem=out_recv.at[h, 1], device_id=(dst, me_c), device_id_type=MESH,
                ).start()

            pltpu.make_async_copy(col_src(me_r), col_dst, out_recv.at[h, 1]).start()

    send_in(0)
    send_in(1)

    @pl.loop(0, H + 2)
    def _(t):
        @pl.when(t < H)
        def _():
            forward(t)

        @pl.when(t < H - 2)
        def _():
            send_in(t + 2)

        @pl.when(jnp.logical_and(t >= 1, t <= H))
        def _():
            merge(t - 1)

        @pl.when(t >= 2)
        def _():
            backward(t - 2)

    def drain(ref, sem):
        pltpu.make_async_copy(ref, ref, sem).wait()

    row_sent = ab.at[:, :, pl.ds(0, K), pl.ds(0, G - COLS)]
    col_sent = ab.at[:, :, pl.ds(0, K), pl.ds(0, G - ROWS)]
    drain(row_sent, in_send.at[0])
    drain(col_sent, in_send.at[1])

    sums = (q_sum, k_sum, v_sum, o_sum)

    def store(h, a):
        return pltpu.make_async_copy(xs.at[h, a], sums[a].at[:, :, h * E:(h + 1) * E], sum_sem.at[h, a])

    for h in range(H - 1):
        drain(row_back.at[h], out_recv.at[h, 0])
        drain(col_back.at[h], out_recv.at[h, 1])
        backs = [
            pltpu.make_async_copy(row_back.at[h], xs.at[h], back_sem.at[h, 0]),
            pltpu.make_async_copy(col_back.at[h], xt.at[h], back_sem.at[h, 1]),
        ]
        for copy in backs:
            copy.start()
        for copy in backs:
            copy.wait()

        @pl.loop(0, COLS // 16)
        def _(cb):
            add_block(perm, xs.at[h], xt.at[h], xs.at[h], cb)

        for a in range(4):
            store(h, a).start()

    for h in range(H - 1):
        for a in range(4):
            store(h, a).wait()
    drain(row_sent, out_send.at[0])
    drain(col_sent, out_send.at[1])
    drain(rs.at[:, pl.ds(0, NC - 1)], stat_send.at[0])
    drain(cs.at[:, pl.ds(0, NR - 1)], stat_send.at[1])
    drain(rr.at[:, pl.ds(0, NC - 1)], merged_send.at[0])
    drain(cr.at[:, pl.ds(0, NR - 1)], merged_send.at[1])
    drain(row_back.at[H - 1], out_recv.at[H - 1, 0])
    drain(col_back.at[H - 1], out_recv.at[H - 1, 1])


def add_block(perm, first, second, total, cb):
    cols = pl.ds(cb * 16 if isinstance(cb, int) else pl.multiple_of(cb * 16, 16), 16)
    for rb in range(ROWS // 16):
        rows = pl.ds(rb * 16, 16)
        for a in range(0, 4, 2):
            pair = [second[a + n, cols, rows, :].reshape(HALF, E) for n in range(2)]
            moved = dot_nn(perm[...], jnp.concatenate(pair, axis=1))
            for n in range(2):
                mine = first[a + n, rows, cols, :].reshape(HALF, E).astype(F32)
                both = (mine + moved[:, n * E:(n + 1) * E]).astype(BF16)
                total[a + n, rows, cols, :] = both.reshape(16, 16, E)


def add_kernel(
    row_back, col_back, q_sum, k_sum, v_sum, o_sum, q_out, k_out, v_out, o_out,
    first, second, stage, perm, back_sem, out_sem, load_sem, store_sem,
):
    sums = (q_sum, k_sum, v_sum, o_sum)
    outs = (q_out, k_out, v_out, o_out)
    backs = [
        pltpu.make_async_copy(row_back.at[H - 1], first, back_sem.at[0]),
        pltpu.make_async_copy(col_back.at[H - 1], second, back_sem.at[1]),
    ]
    for copy in backs:
        copy.start()
    loads = []
    stores = []
    for n in range(MOVES):
        for a in range(4):
            part = (pl.ds(n * (ROWS // MOVES), ROWS // MOVES), slice(None), pl.ds(0, (H - 1) * E))
            here = stage.at[(a,) + part[:2]]
            loads.append(pltpu.make_async_copy(sums[a].at[part], here, load_sem.at[a, n]))
            stores.append(pltpu.make_async_copy(here, outs[a].at[part], store_sem.at[a, n]))
    for copy in loads:
        copy.start()
    perm[...] = swap_matrix()
    for copy in backs:
        copy.wait()
    step = len(loads) // (COLS // 16)
    for cb in range(COLS // 16):
        add_block(perm, first, second, first, cb)
        for n in range(cb * step, cb * step + step):
            loads[n].wait()
            stores[n].start()
    last = [
        pltpu.make_async_copy(first.at[a], outs[a].at[:, :, pl.ds((H - 1) * E, E)], out_sem.at[a])
        for a in range(4)
    ]
    for copy in last:
        copy.start()
    for copy in last + stores:
        copy.wait()


def shards(query_tiles, key_tiles, value_tiles, out_grad):
    any_spec = pl.BlockSpec(memory_space=pl.ANY)
    out = jax.ShapeDtypeStruct((ROWS, COLS, H * E), BF16)
    backs = (
        jax.ShapeDtypeStruct((H, 4, ROWS, COLS, E), BF16),
        jax.ShapeDtypeStruct((H, 4, COLS, ROWS, E), BF16),
    )
    returned = pl.pallas_call(
        kernel,
        out_shape=backs + (out,) * 4,
        in_specs=[any_spec] * 4,
        out_specs=(any_spec,) * 6,
        scratch_shapes=[
            pltpu.VMEM((H, 4, ROWS, COLS, E), BF16),
            pltpu.VMEM((H, 4, COLS, ROWS, E), BF16),
            pltpu.VMEM((H, 4, 2 * K, G, E), BF16),
            pltpu.VMEM((HALF, HALF), BF16),
            pltpu.VMEM((G, E), F32),
            pltpu.VMEM((H, 16, G), F32),
            pltpu.VMEM((H, NC, 8, E), F32),
            pltpu.VMEM((H, NR, 8, E), F32),
            pltpu.VMEM((H, NC, 8, E), F32),
            pltpu.VMEM((H, NR, 8, E), F32),
            pltpu.VMEM((H, NC, 8, E), F32),
            pltpu.VMEM((H, NR, 8, E), F32),
            pltpu.VMEM((16, G), F32),
            pltpu.VMEM((2, ROWS, E), F32),
            pltpu.VMEM((2, E, E), F32),
            pltpu.VMEM((2, E, E), F32),
            pltpu.VMEM((2, E, E), F32),
            pltpu.SemaphoreType.DMA((H, 4)),
            pltpu.SemaphoreType.DMA((2,)),
            pltpu.SemaphoreType.DMA((H, 2)),
            pltpu.SemaphoreType.DMA((2,)),
            pltpu.SemaphoreType.DMA((H, 2)),
            pltpu.SemaphoreType.DMA((2,)),
            pltpu.SemaphoreType.DMA((H, 2)),
            pltpu.SemaphoreType.DMA((2,)),
            pltpu.SemaphoreType.DMA((H, 2)),
            pltpu.SemaphoreType.DMA((H, 2)),
            pltpu.SemaphoreType.DMA((H, 4)),
        ],
        compiler_params=pltpu.CompilerParams(
            collective_id=0, has_side_effects=True, vmem_limit_bytes=52 * 2**20
        ),
        name="attend",
    )(query_tiles, key_tiles, value_tiles, out_grad)
    query_grad, key_grad, value_grad, attended = pl.pallas_call(
        add_kernel,
        out_shape=(out,) * 4,
        in_specs=[any_spec] * 6,
        out_specs=(any_spec,) * 4,
        scratch_shapes=[
            pltpu.VMEM((4, ROWS, COLS, E), BF16),
            pltpu.VMEM((4, COLS, ROWS, E), BF16),
            pltpu.VMEM((4, ROWS, COLS, (H - 1) * E), BF16),
            pltpu.VMEM((HALF, HALF), BF16),
            pltpu.SemaphoreType.DMA((2,)),
            pltpu.SemaphoreType.DMA((4,)),
            pltpu.SemaphoreType.DMA((4, MOVES)),
            pltpu.SemaphoreType.DMA((4, MOVES)),
        ],
        compiler_params=pltpu.CompilerParams(vmem_limit_bytes=60 * 2**20),
        name="add_parts",
    )(*returned)
    return attended, query_grad, key_grad, value_grad


def solution(mesh):
    spec = P("row", "col", None)
    return jax.shard_map(
        shards, mesh=mesh, in_specs=(spec,) * 4, out_specs=(spec,) * 4, check_vma=False
    )
```

```python
import functools

import jax
import jax.numpy as jnp
from jax import lax
from jax.experimental import pallas as pl
from jax.experimental.pallas import tpu as pltpu
from jax.sharding import PartitionSpec as P

H = 4
E = 128
G = 512
ROWS = 32
COLS = 64
NR = 16
NC = 8
K = 4
HALF = 256
LOG2E = 1.4426950408889634
SCALE = E ** (-0.5)
NEG = -1e30
MOVES = 2
MESH = pl.DeviceIdType.MESH
F32 = jnp.float32
BF16 = jnp.bfloat16


def dot_nn(a, b):
    return lax.dot_general(a, b, (((1,), (0,)), ((), ())), preferred_element_type=F32)


def dot_nt(a, b):
    return lax.dot_general(a, b, (((1,), (1,)), ((), ())), preferred_element_type=F32)


def dot_tn(a, b):
    return lax.dot_general(a, b, (((0,), (0,)), ((), ())), preferred_element_type=F32)


def swap_matrix():
    to = lax.broadcasted_iota(jnp.int32, (HALF, HALF), 0)
    of = lax.broadcasted_iota(jnp.int32, (HALF, HALF), 1)
    match = of == (to % 16) * 16 + to // 16
    return jnp.where(match, 1.0, 0.0).astype(BF16)


def kernel(
    q_in, k_in, v_in, g_in, row_back, col_back, q_sum, k_sum, v_sum, o_sum,
    xs, xt, ab, perm, st, so, rs, cs, mr, mc, rr, cr, mm, pr, pc, ct, lt,
    load_sem, in_send, in_recv, out_send, out_recv, stat_send, stat_recv, merged_send, merged_recv,
    back_sem, sum_sem,
):
    me_r = lax.axis_index("row")
    me_c = lax.axis_index("col")
    core = lax.rem(me_c, 2)
    me_z = lax.rem(me_r, 4)
    inputs = (q_in, k_in, v_in, g_in)

    def row_peer(d):
        return lax.rem(me_c + d, NC)

    def col_peer(d):
        return lax.rem(me_r + d, NR)

    def load(h):
        return [
            pltpu.make_async_copy(
                inputs[a].at[:, :, pl.ds(pl.multiple_of(h * E, E), E)], xs.at[h, a], load_sem.at[h, a]
            )
            for a in range(4)
        ]

    def turn(h, a):
        for cb in range(COLS // 16):
            for rb in range(ROWS // 16):
                block = xs[h, a, rb * 16:rb * 16 + 16, cb * 16:cb * 16 + 16, :]
                moved = dot_nn(perm[...], block.reshape(HALF, E)).astype(BF16)
                xt[h, a, cb * 16:cb * 16 + 16, rb * 16:rb * 16 + 16, :] = moved.reshape(16, 16, E)

    for copy in load(0):
        copy.start()

    barrier = pltpu.get_barrier_semaphore()

    @pl.loop(1, NC)
    def _(d):
        pl.semaphore_signal(barrier, inc=1, device_id=(me_r, row_peer(d)), device_id_type=MESH)

    @pl.loop(1, NR)
    def _(d):
        pl.semaphore_signal(barrier, inc=1, device_id=(col_peer(d), me_c), device_id_type=MESH)

    perm[...] = swap_matrix()
    st[...] = jnp.zeros_like(st)
    lt[...] = jnp.zeros_like(lt)
    for copy in load(0):
        copy.wait()
    turn(0, 0)
    pl.semaphore_wait(barrier, NC + NR - 2)

    def send_in(h):
        @pl.when(h > 0)
        def _():
            for copy in load(h):
                copy.wait()

        @pl.when(h < H - 1)
        def _():
            for copy in load(h + 1):
                copy.start()

        def row_src(dst):
            return xs.at[h, :, pl.ds(dst * K, K)]

        row_dst = ab.at[h, :, pl.ds(0, K), pl.ds(pl.multiple_of(me_c * COLS, COLS), COLS)]

        @pl.loop(1, NC)
        def _(d):
            dst = row_peer(d)
            pltpu.make_async_remote_copy(
                src_ref=row_src(dst), dst_ref=row_dst, send_sem=in_send.at[0], recv_sem=in_recv.at[h, 0],
                device_id=(me_r, dst), device_id_type=MESH,
            ).start()

        pltpu.make_async_copy(row_src(me_c), row_dst, in_recv.at[h, 0]).start()

        @pl.loop(0, 4)
        def _(a):
            @pl.when(h + a > 0)
            def _():
                turn(h, a)

            def col_src(dst):
                return xt.at[h, a, pl.ds(dst * K, K)]

            col_dst = ab.at[h, a, pl.ds(K, K), pl.ds(pl.multiple_of(me_r * ROWS, ROWS), ROWS)]

            @pl.loop(1, NR)
            def _(d):
                dst = col_peer(d)
                pltpu.make_async_remote_copy(
                    src_ref=col_src(dst), dst_ref=col_dst, send_sem=in_send.at[1], recv_sem=in_recv.at[h, 1],
                    device_id=(dst, me_c), device_id_type=MESH,
                ).start()

            pltpu.make_async_copy(col_src(me_r), col_dst, in_recv.at[h, 1]).start()

    def forward(h):
        lane = lax.broadcasted_iota(jnp.int32, (HALF, E), 1)
        q_pos = lax.broadcasted_iota(jnp.int32, (HALF, HALF), 0)
        k_pos = lax.broadcasted_iota(jnp.int32, (HALF, HALF), 1)

        for part in range(2):
            here = ab.at[h, :, pl.ds(part * K, K)]
            pltpu.make_async_copy(here, here, in_recv.at[h, part]).wait()

            @pl.loop(0, K)
            def _(k):
                i = part * K + k
                allowed = k_pos <= q_pos - part
                for qb in range(2):
                    rows = pl.ds(qb * HALF, HALF)
                    query = ab[h, 0, i, rows, :]
                    scores = [
                        dot_nt(query, ab[h, 1, i, pl.ds(kb * HALF, HALF), :]) * (SCALE * LOG2E)
                        for kb in range(qb + 1)
                    ]
                    scores[qb] = jnp.where(allowed, scores[qb], NEG)
                    top = scores[0].max(axis=-1, keepdims=True)
                    for s in scores[1:]:
                        top = jnp.maximum(top, s.max(axis=-1, keepdims=True))
                    top = jnp.maximum(top, 0.1 * NEG)
                    weights = [jnp.exp2(s - top) for s in scores]
                    total = weights[0].sum(axis=-1, keepdims=True)
                    for w in weights[1:]:
                        total = total + w.sum(axis=-1, keepdims=True)
                    total = jnp.maximum(total, 1.0)
                    numer = dot_nn(weights[0].astype(BF16), ab[h, 2, i, pl.ds(0, HALF), :])
                    if qb:
                        numer = numer + dot_nn(weights[1].astype(BF16), ab[h, 2, i, pl.ds(HALF, HALF), :])
                    out = (numer / total).astype(BF16).astype(F32)
                    product = (ab[h, 3, i, rows, :].astype(F32) * out).sum(axis=-1, keepdims=True)
                    log_part = top + jnp.log2(total)
                    base = part * 8 + k
                    st[rows, :] = jnp.where(
                        lane == base, log_part, jnp.where(lane == base + 4, product, st[rows, :])
                    )

        for b in range(4):
            block = st[b * E:(b + 1) * E, :].T
            so[h, :, b * E:(b + 1) * E] = block[:16, :]

        def row_stat(dst):
            return so.at[h, pl.ds(0, 8), pl.ds(pl.multiple_of((dst // 2) * E, E), E)]

        def col_stat(dst):
            return so.at[h, pl.ds(8, 8), pl.ds(pl.multiple_of((dst // 4) * E, E), E)]

        @pl.loop(1, NC)
        def _(d):
            dst = row_peer(d)
            pltpu.make_async_remote_copy(
                src_ref=row_stat(dst), dst_ref=rs.at[h, me_c], send_sem=stat_send.at[0],
                recv_sem=stat_recv.at[h, 0], device_id=(me_r, dst), device_id_type=MESH,
            ).start()

        pltpu.make_async_copy(row_stat(me_c), rs.at[h, me_c], stat_recv.at[h, 0]).start()

        @pl.loop(1, NR)
        def _(d):
            dst = col_peer(d)
            pltpu.make_async_remote_copy(
                src_ref=col_stat(dst), dst_ref=cs.at[h, me_r], send_sem=stat_send.at[1],
                recv_sem=stat_recv.at[h, 1], device_id=(dst, me_c), device_id_type=MESH,
            ).start()

        pltpu.make_async_copy(col_stat(me_r), cs.at[h, me_r], stat_recv.at[h, 1]).start()

    def merge(h):
        pltpu.make_async_copy(rs.at[h], rs.at[h], stat_recv.at[h, 0]).wait()
        pltpu.make_async_copy(cs.at[h], cs.at[h], stat_recv.at[h, 1]).wait()
        row_values = []
        col_values = []
        for s in range(2):
            for d in range(NC):
                pr[s, 4 * d:4 * d + 4, :] = rs[h, d, 4 * s:4 * s + 4, :]
            for j in range(NR):
                pc[s, 4 * j:4 * j + 4, :] = cs[h, j, 4 * s:4 * s + 4, :]
                pc[s, COLS + 4 * j:COLS + 4 * j + 4, :] = cs[h, j, 4 * s:4 * s + 4, :]
            ct[s] = pc[s].T
            row_values.append(pr[s])
            col_values.append(ct[s, pl.ds(pl.multiple_of(me_z * ROWS, ROWS), ROWS), :])
        top = jnp.maximum(row_values[0], col_values[0])
        log_total = top + jnp.log2(jnp.exp2(row_values[0] - top) + jnp.exp2(col_values[0] - top))
        delta = (
            jnp.exp2(row_values[0] - log_total) * row_values[1]
            + jnp.exp2(col_values[0] - log_total) * col_values[1]
        )
        for s, value in enumerate((log_total, delta)):
            pr[s] = value
            lt[s, pl.ds(pl.multiple_of(me_z * ROWS, ROWS), ROWS), :] = value
            turned = lt[s].T
            pc[s, :COLS, :] = jnp.where(core == 0, turned[:COLS], turned[COLS:])
            for d in range(NC):
                mr[h, d, 4 * s:4 * s + 4, :] = pr[s, 4 * d:4 * d + 4, :]
            for j in range(NR):
                mc[h, j, 4 * s:4 * s + 4, :] = pc[s, 4 * j:4 * j + 4, :]

        @pl.loop(1, NC)
        def _(d):
            dst = row_peer(d)
            pltpu.make_async_remote_copy(
                src_ref=mr.at[h, dst], dst_ref=rr.at[h, me_c], send_sem=merged_send.at[0],
                recv_sem=merged_recv.at[h, 0], device_id=(me_r, dst), device_id_type=MESH,
            ).start()

        pltpu.make_async_copy(mr.at[h, me_c], rr.at[h, me_c], merged_recv.at[h, 0]).start()

        @pl.loop(1, NR)
        def _(d):
            dst = col_peer(d)
            pltpu.make_async_remote_copy(
                src_ref=mc.at[h, dst], dst_ref=cr.at[h, me_r], send_sem=merged_send.at[1],
                recv_sem=merged_recv.at[h, 1], device_id=(dst, me_c), device_id_type=MESH,
            ).start()

        pltpu.make_async_copy(mc.at[h, me_r], cr.at[h, me_r], merged_recv.at[h, 1]).start()

    def backward(h):
        pltpu.make_async_copy(rr.at[h], rr.at[h], merged_recv.at[h, 0]).wait()
        pltpu.make_async_copy(cr.at[h], cr.at[h], merged_recv.at[h, 1]).wait()
        lane = lax.broadcasted_iota(jnp.int32, (8, E), 1)
        for y in range(4):
            mm[0:8, y * E:(y + 1) * E] = jnp.where(lane < COLS, rr[h, 2 * y], rr[h, 2 * y + 1])
            tile = cr[h, 4 * y]
            for z in range(1, 4):
                tile = jnp.where(lane >= z * ROWS, cr[h, 4 * y + z], tile)
            mm[8:16, y * E:(y + 1) * E] = tile

        k_pos = lax.broadcasted_iota(jnp.int32, (HALF, HALF), 0)
        q_pos = lax.broadcasted_iota(jnp.int32, (HALF, HALF), 1)

        def instance(part, k):
            i = part * K + k
            allowed = k_pos <= q_pos - part
            key_grads = [None, None]
            value_grads = [None, None]
            for qb in range(2):
                rows = pl.ds(qb * HALF, HALF)
                query = ab[h, 0, i, rows, :]
                grad = ab[h, 3, i, rows, :]
                log_total = mm[pl.ds(part * 8 + k, 1), rows]
                delta = mm[pl.ds(part * 8 + 4 + k, 1), rows]
                query_grad = None
                out = None
                for kb in range(qb + 1):
                    keys = ab[h, 1, i, pl.ds(kb * HALF, HALF), :]
                    values = ab[h, 2, i, pl.ds(kb * HALF, HALF), :]
                    scores = dot_nt(keys, query) * (SCALE * LOG2E)
                    if kb == qb:
                        scores = jnp.where(allowed, scores, NEG)
                    probs = jnp.exp2(scores - log_total)
                    score_grad = probs * (dot_nt(values, grad) - delta)
                    probs_half = probs.astype(BF16)
                    score_half = score_grad.astype(BF16)
                    terms = (
                        dot_nn(score_half, query), dot_nn(probs_half, grad),
                        dot_tn(keys, score_half), dot_tn(values, probs_half),
                    )
                    if kb < qb:
                        key_grads[kb] = key_grads[kb] + terms[0]
                        value_grads[kb] = value_grads[kb] + terms[1]
                    else:
                        key_grads[kb] = terms[0]
                        value_grads[kb] = terms[1]
                    query_grad = terms[2] if query_grad is None else query_grad + terms[2]
                    out = terms[3] if out is None else out + terms[3]
                ab[h, 0, i, rows, :] = (query_grad * SCALE).T.astype(BF16)
                ab[h, 3, i, rows, :] = out.T.astype(BF16)
            for kb in range(2):
                where = pl.ds(kb * HALF, HALF)
                ab[h, 1, i, where, :] = (key_grads[kb] * SCALE).astype(BF16)
                ab[h, 2, i, where, :] = value_grads[kb].astype(BF16)

        @pl.loop(0, K)
        def _(k):
            instance(1, k)

            def col_src(dst):
                return ab.at[h, :, K + k, pl.ds(pl.multiple_of(dst * ROWS, ROWS), ROWS)]

            col_dst = col_back.at[h, :, me_r * K + k]

            @pl.loop(1, NR)
            def _(d):
                dst = col_peer(d)
                pltpu.make_async_remote_copy(
                    src_ref=col_src(dst), dst_ref=col_dst, send_sem=out_send.at[1],
                    recv_sem=out_recv.at[h, 1], device_id=(dst, me_c), device_id_type=MESH,
                ).start()

            pltpu.make_async_copy(col_src(me_r), col_dst, out_recv.at[h, 1]).start()
            instance(0, k)

            def row_src(dst):
                return ab.at[h, :, k, pl.ds(pl.multiple_of(dst * COLS, COLS), COLS)]

            row_dst = row_back.at[h, :, me_c * K + k]

            @pl.loop(1, NC)
            def _(d):
                dst = row_peer(d)
                pltpu.make_async_remote_copy(
                    src_ref=row_src(dst), dst_ref=row_dst, send_sem=out_send.at[0],
                    recv_sem=out_recv.at[h, 0], device_id=(me_r, dst), device_id_type=MESH,
                ).start()

            pltpu.make_async_copy(row_src(me_c), row_dst, out_recv.at[h, 0]).start()

    send_in(0)
    send_in(1)

    @pl.loop(0, H + 2)
    def _(t):
        @pl.when(t < H)
        def _():
            forward(t)

        @pl.when(t < H - 2)
        def _():
            send_in(t + 2)

        @pl.when(jnp.logical_and(t >= 1, t <= H))
        def _():
            merge(t - 1)

        @pl.when(t >= 2)
        def _():
            backward(t - 2)

    def drain(ref, sem):
        pltpu.make_async_copy(ref, ref, sem).wait()

    row_sent = ab.at[:, :, pl.ds(0, K), pl.ds(0, G - COLS)]
    col_sent = ab.at[:, :, pl.ds(0, K), pl.ds(0, G - ROWS)]
    drain(row_sent, in_send.at[0])
    drain(col_sent, in_send.at[1])

    sums = (q_sum, k_sum, v_sum, o_sum)

    def store(h, a):
        return pltpu.make_async_copy(xs.at[h, a], sums[a].at[:, :, h * E:(h + 1) * E], sum_sem.at[h, a])

    for h in range(H - 1):
        drain(row_back.at[h], out_recv.at[h, 0])
        drain(col_back.at[h], out_recv.at[h, 1])
        backs = [
            pltpu.make_async_copy(row_back.at[h], xs.at[h], back_sem.at[h, 0]),
            pltpu.make_async_copy(col_back.at[h], xt.at[h], back_sem.at[h, 1]),
        ]
        for copy in backs:
            copy.start()
        for copy in backs:
            copy.wait()

        @pl.loop(0, COLS // 16)
        def _(cb):
            add_block(perm, xs.at[h], xt.at[h], xs.at[h], cb)

        for a in range(4):
            store(h, a).start()

    for h in range(H - 1):
        for a in range(4):
            store(h, a).wait()
    drain(row_sent, out_send.at[0])
    drain(col_sent, out_send.at[1])
    drain(rs.at[:, pl.ds(0, NC - 1)], stat_send.at[0])
    drain(cs.at[:, pl.ds(0, NR - 1)], stat_send.at[1])
    drain(rr.at[:, pl.ds(0, NC - 1)], merged_send.at[0])
    drain(cr.at[:, pl.ds(0, NR - 1)], merged_send.at[1])
    drain(row_back.at[H - 1], out_recv.at[H - 1, 0])
    drain(col_back.at[H - 1], out_recv.at[H - 1, 1])


def add_block(perm, first, second, total, cb):
    cols = pl.ds(cb * 16 if isinstance(cb, int) else pl.multiple_of(cb * 16, 16), 16)
    for rb in range(ROWS // 16):
        rows = pl.ds(rb * 16, 16)
        for a in range(0, 4, 2):
            pair = [second[a + n, cols, rows, :].reshape(HALF, E) for n in range(2)]
            moved = dot_nn(perm[...], jnp.concatenate(pair, axis=1))
            for n in range(2):
                mine = first[a + n, rows, cols, :].reshape(HALF, E).astype(F32)
                both = (mine + moved[:, n * E:(n + 1) * E]).astype(BF16)
                total[a + n, rows, cols, :] = both.reshape(16, 16, E)


def add_kernel(
    row_back, col_back, q_sum, k_sum, v_sum, o_sum, q_out, k_out, v_out, o_out,
    first, second, stage, perm, back_sem, out_sem, load_sem, store_sem,
):
    sums = (q_sum, k_sum, v_sum, o_sum)
    outs = (q_out, k_out, v_out, o_out)
    backs = [
        pltpu.make_async_copy(row_back.at[H - 1], first, back_sem.at[0]),
        pltpu.make_async_copy(col_back.at[H - 1], second, back_sem.at[1]),
    ]
    for copy in backs:
        copy.start()
    loads = []
    stores = []
    for n in range(MOVES):
        for a in range(4):
            part = (pl.ds(n * (ROWS // MOVES), ROWS // MOVES), slice(None), pl.ds(0, (H - 1) * E))
            here = stage.at[(a,) + part[:2]]
            loads.append(pltpu.make_async_copy(sums[a].at[part], here, load_sem.at[a, n]))
            stores.append(pltpu.make_async_copy(here, outs[a].at[part], store_sem.at[a, n]))
    for copy in loads:
        copy.start()
    perm[...] = swap_matrix()
    for copy in backs:
        copy.wait()
    step = len(loads) // (COLS // 16)
    for cb in range(COLS // 16):
        add_block(perm, first, second, first, cb)
        for n in range(cb * step, cb * step + step):
            loads[n].wait()
            stores[n].start()
    last = [
        pltpu.make_async_copy(first.at[a], outs[a].at[:, :, pl.ds((H - 1) * E, E)], out_sem.at[a])
        for a in range(4)
    ]
    for copy in last:
        copy.start()
    for copy in last + stores:
        copy.wait()


def shards(query_tiles, key_tiles, value_tiles, out_grad):
    any_spec = pl.BlockSpec(memory_space=pl.ANY)
    out = jax.ShapeDtypeStruct((ROWS, COLS, H * E), BF16)
    backs = (
        jax.ShapeDtypeStruct((H, 4, ROWS, COLS, E), BF16),
        jax.ShapeDtypeStruct((H, 4, COLS, ROWS, E), BF16),
    )
    returned = pl.pallas_call(
        kernel,
        out_shape=backs + (out,) * 4,
        in_specs=[any_spec] * 4,
        out_specs=(any_spec,) * 6,
        scratch_shapes=[
            pltpu.VMEM((H, 4, ROWS, COLS, E), BF16),
            pltpu.VMEM((H, 4, COLS, ROWS, E), BF16),
            pltpu.VMEM((H, 4, 2 * K, G, E), BF16),
            pltpu.VMEM((HALF, HALF), BF16),
            pltpu.VMEM((G, E), F32),
            pltpu.VMEM((H, 16, G), F32),
            pltpu.VMEM((H, NC, 8, E), F32),
            pltpu.VMEM((H, NR, 8, E), F32),
            pltpu.VMEM((H, NC, 8, E), F32),
            pltpu.VMEM((H, NR, 8, E), F32),
            pltpu.VMEM((H, NC, 8, E), F32),
            pltpu.VMEM((H, NR, 8, E), F32),
            pltpu.VMEM((16, G), F32),
            pltpu.VMEM((2, ROWS, E), F32),
            pltpu.VMEM((2, E, E), F32),
            pltpu.VMEM((2, E, E), F32),
            pltpu.VMEM((2, E, E), F32),
            pltpu.SemaphoreType.DMA((H, 4)),
            pltpu.SemaphoreType.DMA((2,)),
            pltpu.SemaphoreType.DMA((H, 2)),
            pltpu.SemaphoreType.DMA((2,)),
            pltpu.SemaphoreType.DMA((H, 2)),
            pltpu.SemaphoreType.DMA((2,)),
            pltpu.SemaphoreType.DMA((H, 2)),
            pltpu.SemaphoreType.DMA((2,)),
            pltpu.SemaphoreType.DMA((H, 2)),
            pltpu.SemaphoreType.DMA((H, 2)),
            pltpu.SemaphoreType.DMA((H, 4)),
        ],
        compiler_params=pltpu.CompilerParams(
            collective_id=0, has_side_effects=True, vmem_limit_bytes=52 * 2**20
        ),
        name="attend",
    )(query_tiles, key_tiles, value_tiles, out_grad)
    query_grad, key_grad, value_grad, attended = pl.pallas_call(
        add_kernel,
        out_shape=(out,) * 4,
        in_specs=[any_spec] * 6,
        out_specs=(any_spec,) * 4,
        scratch_shapes=[
            pltpu.VMEM((4, ROWS, COLS, E), BF16),
            pltpu.VMEM((4, COLS, ROWS, E), BF16),
            pltpu.VMEM((4, ROWS, COLS, (H - 1) * E), BF16),
            pltpu.VMEM((HALF, HALF), BF16),
            pltpu.SemaphoreType.DMA((2,)),
            pltpu.SemaphoreType.DMA((4,)),
            pltpu.SemaphoreType.DMA((4, MOVES)),
            pltpu.SemaphoreType.DMA((4, MOVES)),
        ],
        compiler_params=pltpu.CompilerParams(vmem_limit_bytes=60 * 2**20),
        name="add_parts",
    )(*returned)
    return attended, query_grad, key_grad, value_grad


def solution(mesh):
    spec = P("row", "col", None)
    return jax.shard_map(
        shards, mesh=mesh, in_specs=(spec,) * 4, out_specs=(spec,) * 4, check_vma=False
    )
```

```python
import functools

import jax
import jax.numpy as jnp
from jax import lax
from jax.experimental import pallas as pl
from jax.experimental.pallas import tpu as pltpu
from jax.sharding import PartitionSpec as P

H = 4
E = 128
G = 512
ROWS = 32
COLS = 64
NR = 16
NC = 8
K = 4
HALF = 256
LOG2E = 1.4426950408889634
SCALE = E ** (-0.5)
NEG = -1e30
MOVES = 1
MESH = pl.DeviceIdType.MESH
F32 = jnp.float32
BF16 = jnp.bfloat16


def dot_nn(a, b):
    return lax.dot_general(a, b, (((1,), (0,)), ((), ())), preferred_element_type=F32)


def dot_nt(a, b):
    return lax.dot_general(a, b, (((1,), (1,)), ((), ())), preferred_element_type=F32)


def dot_tn(a, b):
    return lax.dot_general(a, b, (((0,), (0,)), ((), ())), preferred_element_type=F32)


def swap_matrix():
    to = lax.broadcasted_iota(jnp.int32, (HALF, HALF), 0)
    of = lax.broadcasted_iota(jnp.int32, (HALF, HALF), 1)
    match = of == (to % 16) * 16 + to // 16
    return jnp.where(match, 1.0, 0.0).astype(BF16)


def kernel(
    q_in, k_in, v_in, g_in, row_back, col_back, q_sum, k_sum, v_sum, o_sum,
    xs, xt, ab, perm, st, so, rs, cs, mr, mc, rr, cr, mm, pr, pc, ct, lt,
    load_sem, in_send, in_recv, out_send, out_recv, stat_send, stat_recv, merged_send, merged_recv,
    back_sem, sum_sem,
):
    me_r = lax.axis_index("row")
    me_c = lax.axis_index("col")
    core = lax.rem(me_c, 2)
    me_z = lax.rem(me_r, 4)
    inputs = (q_in, k_in, v_in, g_in)

    def row_peer(d):
        return lax.rem(me_c + d, NC)

    def col_peer(d):
        return lax.rem(me_r + d, NR)

    def load(h):
        return [
            pltpu.make_async_copy(
                inputs[a].at[:, :, pl.ds(pl.multiple_of(h * E, E), E)], xs.at[h, a], load_sem.at[h, a]
            )
            for a in range(4)
        ]

    def turn(h, a):
        for cb in range(COLS // 16):
            for rb in range(ROWS // 16):
                block = xs[h, a, rb * 16:rb * 16 + 16, cb * 16:cb * 16 + 16, :]
                moved = dot_nn(perm[...], block.reshape(HALF, E)).astype(BF16)
                xt[h, a, cb * 16:cb * 16 + 16, rb * 16:rb * 16 + 16, :] = moved.reshape(16, 16, E)

    for copy in load(0):
        copy.start()

    barrier = pltpu.get_barrier_semaphore()

    @pl.loop(1, NC)
    def _(d):
        pl.semaphore_signal(barrier, inc=1, device_id=(me_r, row_peer(d)), device_id_type=MESH)

    @pl.loop(1, NR)
    def _(d):
        pl.semaphore_signal(barrier, inc=1, device_id=(col_peer(d), me_c), device_id_type=MESH)

    perm[...] = swap_matrix()
    st[...] = jnp.zeros_like(st)
    lt[...] = jnp.zeros_like(lt)
    for copy in load(0):
        copy.wait()
    turn(0, 0)
    pl.semaphore_wait(barrier, NC + NR - 2)

    def send_in(h):
        @pl.when(h > 0)
        def _():
            for copy in load(h):
                copy.wait()

        @pl.when(h < H - 1)
        def _():
            for copy in load(h + 1):
                copy.start()

        def row_src(dst):
            return xs.at[h, :, pl.ds(dst * K, K)]

        row_dst = ab.at[h, :, pl.ds(0, K), pl.ds(pl.multiple_of(me_c * COLS, COLS), COLS)]

        @pl.loop(0, 4)
        def _(a):
            @pl.when(h + a > 0)
            def _():
                turn(h, a)

            def col_src(dst):
                return xt.at[h, a, pl.ds(dst * K, K)]

            col_dst = ab.at[h, a, pl.ds(K, K), pl.ds(pl.multiple_of(me_r * ROWS, ROWS), ROWS)]

            @pl.loop(1, NR)
            def _(d):
                dst = col_peer(d)
                pltpu.make_async_remote_copy(
                    src_ref=col_src(dst), dst_ref=col_dst, send_sem=in_send.at[1], recv_sem=in_recv.at[h, 1],
                    device_id=(dst, me_c), device_id_type=MESH,
                ).start()

            pltpu.make_async_copy(col_src(me_r), col_dst, in_recv.at[h, 1]).start()

            @pl.when(a == 0)
            def _():
                @pl.loop(1, NC)
                def _(d):
                    dst = row_peer(d)
                    pltpu.make_async_remote_copy(
                        src_ref=row_src(dst), dst_ref=row_dst, send_sem=in_send.at[0], recv_sem=in_recv.at[h, 0],
                        device_id=(me_r, dst), device_id_type=MESH,
                    ).start()

                pltpu.make_async_copy(row_src(me_c), row_dst, in_recv.at[h, 0]).start()

    def forward(h):
        lane = lax.broadcasted_iota(jnp.int32, (HALF, E), 1)
        q_pos = lax.broadcasted_iota(jnp.int32, (HALF, HALF), 0)
        k_pos = lax.broadcasted_iota(jnp.int32, (HALF, HALF), 1)

        for part in range(2):
            here = ab.at[h, :, pl.ds(part * K, K)]
            pltpu.make_async_copy(here, here, in_recv.at[h, part]).wait()

            @pl.loop(0, K)
            def _(k):
                i = part * K + k
                allowed = k_pos <= q_pos - part
                for qb in range(2):
                    rows = pl.ds(qb * HALF, HALF)
                    query = ab[h, 0, i, rows, :]
                    scores = [
                        dot_nt(query, ab[h, 1, i, pl.ds(kb * HALF, HALF), :]) * (SCALE * LOG2E)
                        for kb in range(qb + 1)
                    ]
                    scores[qb] = jnp.where(allowed, scores[qb], NEG)
                    top = scores[0].max(axis=-1, keepdims=True)
                    for s in scores[1:]:
                        top = jnp.maximum(top, s.max(axis=-1, keepdims=True))
                    top = jnp.maximum(top, 0.1 * NEG)
                    weights = [jnp.exp2(s - top) for s in scores]
                    total = weights[0].sum(axis=-1, keepdims=True)
                    for w in weights[1:]:
                        total = total + w.sum(axis=-1, keepdims=True)
                    total = jnp.maximum(total, 1.0)
                    numer = dot_nn(weights[0].astype(BF16), ab[h, 2, i, pl.ds(0, HALF), :])
                    if qb:
                        numer = numer + dot_nn(weights[1].astype(BF16), ab[h, 2, i, pl.ds(HALF, HALF), :])
                    out = (numer / total).astype(BF16).astype(F32)
                    product = (ab[h, 3, i, rows, :].astype(F32) * out).sum(axis=-1, keepdims=True)
                    log_part = top + jnp.log2(total)
                    base = part * 8 + k
                    st[rows, :] = jnp.where(
                        lane == base, log_part, jnp.where(lane == base + 4, product, st[rows, :])
                    )

        for b in range(4):
            block = st[b * E:(b + 1) * E, :].T
            so[h, :, b * E:(b + 1) * E] = block[:16, :]

        def row_stat(dst):
            return so.at[h, pl.ds(0, 8), pl.ds(pl.multiple_of((dst // 2) * E, E), E)]

        def col_stat(dst):
            return so.at[h, pl.ds(8, 8), pl.ds(pl.multiple_of((dst // 4) * E, E), E)]

        @pl.loop(1, NC)
        def _(d):
            dst = row_peer(d)
            pltpu.make_async_remote_copy(
                src_ref=row_stat(dst), dst_ref=rs.at[h, me_c], send_sem=stat_send.at[0],
                recv_sem=stat_recv.at[h, 0], device_id=(me_r, dst), device_id_type=MESH,
            ).start()

        pltpu.make_async_copy(row_stat(me_c), rs.at[h, me_c], stat_recv.at[h, 0]).start()

        @pl.loop(1, NR)
        def _(d):
            dst = col_peer(d)
            pltpu.make_async_remote_copy(
                src_ref=col_stat(dst), dst_ref=cs.at[h, me_r], send_sem=stat_send.at[1],
                recv_sem=stat_recv.at[h, 1], device_id=(dst, me_c), device_id_type=MESH,
            ).start()

        pltpu.make_async_copy(col_stat(me_r), cs.at[h, me_r], stat_recv.at[h, 1]).start()

    def merge(h):
        pltpu.make_async_copy(rs.at[h], rs.at[h], stat_recv.at[h, 0]).wait()
        pltpu.make_async_copy(cs.at[h], cs.at[h], stat_recv.at[h, 1]).wait()
        row_values = []
        col_values = []
        for s in range(2):
            for d in range(NC):
                pr[s, 4 * d:4 * d + 4, :] = rs[h, d, 4 * s:4 * s + 4, :]
            for j in range(NR):
                pc[s, 4 * j:4 * j + 4, :] = cs[h, j, 4 * s:4 * s + 4, :]
                pc[s, COLS + 4 * j:COLS + 4 * j + 4, :] = cs[h, j, 4 * s:4 * s + 4, :]
            ct[s] = pc[s].T
            row_values.append(pr[s])
            col_values.append(ct[s, pl.ds(pl.multiple_of(me_z * ROWS, ROWS), ROWS), :])
        top = jnp.maximum(row_values[0], col_values[0])
        log_total = top + jnp.log2(jnp.exp2(row_values[0] - top) + jnp.exp2(col_values[0] - top))
        delta = (
            jnp.exp2(row_values[0] - log_total) * row_values[1]
            + jnp.exp2(col_values[0] - log_total) * col_values[1]
        )
        for s, value in enumerate((log_total, delta)):
            pr[s] = value
            lt[s, pl.ds(pl.multiple_of(me_z * ROWS, ROWS), ROWS), :] = value
            turned = lt[s].T
            pc[s, :COLS, :] = jnp.where(core == 0, turned[:COLS], turned[COLS:])
            for d in range(NC):
                mr[h, d, 4 * s:4 * s + 4, :] = pr[s, 4 * d:4 * d + 4, :]
            for j in range(NR):
                mc[h, j, 4 * s:4 * s + 4, :] = pc[s, 4 * j:4 * j + 4, :]

        @pl.loop(1, NC)
        def _(d):
            dst = row_peer(d)
            pltpu.make_async_remote_copy(
                src_ref=mr.at[h, dst], dst_ref=rr.at[h, me_c], send_sem=merged_send.at[0],
                recv_sem=merged_recv.at[h, 0], device_id=(me_r, dst), device_id_type=MESH,
            ).start()

        pltpu.make_async_copy(mr.at[h, me_c], rr.at[h, me_c], merged_recv.at[h, 0]).start()

        @pl.loop(1, NR)
        def _(d):
            dst = col_peer(d)
            pltpu.make_async_remote_copy(
                src_ref=mc.at[h, dst], dst_ref=cr.at[h, me_r], send_sem=merged_send.at[1],
                recv_sem=merged_recv.at[h, 1], device_id=(dst, me_c), device_id_type=MESH,
            ).start()

        pltpu.make_async_copy(mc.at[h, me_r], cr.at[h, me_r], merged_recv.at[h, 1]).start()

    def backward(h):
        pltpu.make_async_copy(rr.at[h], rr.at[h], merged_recv.at[h, 0]).wait()
        pltpu.make_async_copy(cr.at[h], cr.at[h], merged_recv.at[h, 1]).wait()
        lane = lax.broadcasted_iota(jnp.int32, (8, E), 1)
        for y in range(4):
            mm[0:8, y * E:(y + 1) * E] = jnp.where(lane < COLS, rr[h, 2 * y], rr[h, 2 * y + 1])
            tile = cr[h, 4 * y]
            for z in range(1, 4):
                tile = jnp.where(lane >= z * ROWS, cr[h, 4 * y + z], tile)
            mm[8:16, y * E:(y + 1) * E] = tile

        k_pos = lax.broadcasted_iota(jnp.int32, (HALF, HALF), 0)
        q_pos = lax.broadcasted_iota(jnp.int32, (HALF, HALF), 1)

        def instance(part, k):
            i = part * K + k
            allowed = k_pos <= q_pos - part
            key_grads = [None, None]
            value_grads = [None, None]
            for qb in range(2):
                rows = pl.ds(qb * HALF, HALF)
                query = ab[h, 0, i, rows, :]
                grad = ab[h, 3, i, rows, :]
                log_total = mm[pl.ds(part * 8 + k, 1), rows]
                delta = mm[pl.ds(part * 8 + 4 + k, 1), rows]
                query_grad = None
                out = None
                for kb in range(qb + 1):
                    keys = ab[h, 1, i, pl.ds(kb * HALF, HALF), :]
                    values = ab[h, 2, i, pl.ds(kb * HALF, HALF), :]
                    scores = dot_nt(keys, query) * (SCALE * LOG2E)
                    if kb == qb:
                        scores = jnp.where(allowed, scores, NEG)
                    probs = jnp.exp2(scores - log_total)
                    score_grad = probs * (dot_nt(values, grad) - delta)
                    probs_half = probs.astype(BF16)
                    score_half = score_grad.astype(BF16)
                    terms = (
                        dot_nn(score_half, query), dot_nn(probs_half, grad),
                        dot_tn(keys, score_half), dot_tn(values, probs_half),
                    )
                    if kb < qb:
                        key_grads[kb] = key_grads[kb] + terms[0]
                        value_grads[kb] = value_grads[kb] + terms[1]
                    else:
                        key_grads[kb] = terms[0]
                        value_grads[kb] = terms[1]
                    query_grad = terms[2] if query_grad is None else query_grad + terms[2]
                    out = terms[3] if out is None else out + terms[3]
                ab[h, 0, i, rows, :] = (query_grad * SCALE).T.astype(BF16)
                ab[h, 3, i, rows, :] = out.T.astype(BF16)
            for kb in range(2):
                where = pl.ds(kb * HALF, HALF)
                ab[h, 1, i, where, :] = (key_grads[kb] * SCALE).astype(BF16)
                ab[h, 2, i, where, :] = value_grads[kb].astype(BF16)

        @pl.loop(0, K)
        def _(k):
            instance(1, k)

            def col_src(dst):
                return ab.at[h, :, K + k, pl.ds(pl.multiple_of(dst * ROWS, ROWS), ROWS)]

            col_dst = col_back.at[h, :, me_r * K + k]

            @pl.loop(1, NR)
            def _(d):
                dst = col_peer(d)
                pltpu.make_async_remote_copy(
                    src_ref=col_src(dst), dst_ref=col_dst, send_sem=out_send.at[1],
                    recv_sem=out_recv.at[h, 1], device_id=(dst, me_c), device_id_type=MESH,
                ).start()

            pltpu.make_async_copy(col_src(me_r), col_dst, out_recv.at[h, 1]).start()
            instance(0, k)

            def row_src(dst):
                return ab.at[h, :, k, pl.ds(pl.multiple_of(dst * COLS, COLS), COLS)]

            row_dst = row_back.at[h, :, me_c * K + k]

            @pl.loop(1, NC)
            def _(d):
                dst = row_peer(d)
                pltpu.make_async_remote_copy(
                    src_ref=row_src(dst), dst_ref=row_dst, send_sem=out_send.at[0],
                    recv_sem=out_recv.at[h, 0], device_id=(me_r, dst), device_id_type=MESH,
                ).start()

            pltpu.make_async_copy(row_src(me_c), row_dst, out_recv.at[h, 0]).start()

    send_in(0)
    send_in(1)

    @pl.loop(0, H + 2)
    def _(t):
        @pl.when(t < H)
        def _():
            forward(t)

        @pl.when(t < H - 2)
        def _():
            send_in(t + 2)

        @pl.when(jnp.logical_and(t >= 1, t <= H))
        def _():
            merge(t - 1)

        @pl.when(t >= 2)
        def _():
            backward(t - 2)

    def drain(ref, sem):
        pltpu.make_async_copy(ref, ref, sem).wait()

    row_sent = ab.at[:, :, pl.ds(0, K), pl.ds(0, G - COLS)]
    col_sent = ab.at[:, :, pl.ds(0, K), pl.ds(0, G - ROWS)]
    drain(row_sent, in_send.at[0])
    drain(col_sent, in_send.at[1])

    sums = (q_sum, k_sum, v_sum, o_sum)

    def store(h, a):
        return pltpu.make_async_copy(xs.at[h, a], sums[a].at[:, :, h * E:(h + 1) * E], sum_sem.at[h, a])

    for h in range(H - 1):
        drain(row_back.at[h], out_recv.at[h, 0])
        drain(col_back.at[h], out_recv.at[h, 1])
        backs = [
            pltpu.make_async_copy(row_back.at[h], xs.at[h], back_sem.at[h, 0]),
            pltpu.make_async_copy(col_back.at[h], xt.at[h], back_sem.at[h, 1]),
        ]
        for copy in backs:
            copy.start()
        for copy in backs:
            copy.wait()

        @pl.loop(0, COLS // 16)
        def _(cb):
            add_block(perm, xs.at[h], xt.at[h], xs.at[h], cb)

        for a in range(4):
            store(h, a).start()

    for h in range(H - 1):
        for a in range(4):
            store(h, a).wait()
    drain(row_sent, out_send.at[0])
    drain(col_sent, out_send.at[1])
    drain(rs.at[:, pl.ds(0, NC - 1)], stat_send.at[0])
    drain(cs.at[:, pl.ds(0, NR - 1)], stat_send.at[1])
    drain(rr.at[:, pl.ds(0, NC - 1)], merged_send.at[0])
    drain(cr.at[:, pl.ds(0, NR - 1)], merged_send.at[1])
    drain(row_back.at[H - 1], out_recv.at[H - 1, 0])
    drain(col_back.at[H - 1], out_recv.at[H - 1, 1])


def add_block(perm, first, second, total, cb):
    cols = pl.ds(cb * 16 if isinstance(cb, int) else pl.multiple_of(cb * 16, 16), 16)
    for rb in range(ROWS // 16):
        rows = pl.ds(rb * 16, 16)
        for a in range(0, 4, 2):
            pair = [second[a + n, cols, rows, :].reshape(HALF, E) for n in range(2)]
            moved = dot_nn(perm[...], jnp.concatenate(pair, axis=1))
            for n in range(2):
                mine = first[a + n, rows, cols, :].reshape(HALF, E).astype(F32)
                both = (mine + moved[:, n * E:(n + 1) * E]).astype(BF16)
                total[a + n, rows, cols, :] = both.reshape(16, 16, E)


def add_kernel(
    row_back, col_back, q_sum, k_sum, v_sum, o_sum, q_out, k_out, v_out, o_out,
    first, second, stage, perm, back_sem, out_sem, load_sem, store_sem,
):
    sums = (q_sum, k_sum, v_sum, o_sum)
    outs = (q_out, k_out, v_out, o_out)
    backs = [
        pltpu.make_async_copy(row_back.at[H - 1], first, back_sem.at[0]),
        pltpu.make_async_copy(col_back.at[H - 1], second, back_sem.at[1]),
    ]
    for copy in backs:
        copy.start()
    loads = []
    stores = []
    for n in range(MOVES):
        for a in range(4):
            part = (pl.ds(n * (ROWS // MOVES), ROWS // MOVES), slice(None), pl.ds(0, (H - 1) * E))
            here = stage.at[(a,) + part[:2]]
            loads.append(pltpu.make_async_copy(sums[a].at[part], here, load_sem.at[a, n]))
            stores.append(pltpu.make_async_copy(here, outs[a].at[part], store_sem.at[a, n]))
    for copy in loads:
        copy.start()
    perm[...] = swap_matrix()
    for copy in backs:
        copy.wait()
    step = len(loads) // (COLS // 16)
    for cb in range(COLS // 16):
        add_block(perm, first, second, first, cb)
        for n in range(cb * step, cb * step + step):
            loads[n].wait()
            stores[n].start()
    last = [
        pltpu.make_async_copy(first.at[a], outs[a].at[:, :, pl.ds((H - 1) * E, E)], out_sem.at[a])
        for a in range(4)
    ]
    for copy in last:
        copy.start()
    for copy in last + stores:
        copy.wait()


def shards(query_tiles, key_tiles, value_tiles, out_grad):
    any_spec = pl.BlockSpec(memory_space=pl.ANY)
    out = jax.ShapeDtypeStruct((ROWS, COLS, H * E), BF16)
    backs = (
        jax.ShapeDtypeStruct((H, 4, ROWS, COLS, E), BF16),
        jax.ShapeDtypeStruct((H, 4, COLS, ROWS, E), BF16),
    )
    returned = pl.pallas_call(
        kernel,
        out_shape=backs + (out,) * 4,
        in_specs=[any_spec] * 4,
        out_specs=(any_spec,) * 6,
        scratch_shapes=[
            pltpu.VMEM((H, 4, ROWS, COLS, E), BF16),
            pltpu.VMEM((H, 4, COLS, ROWS, E), BF16),
            pltpu.VMEM((H, 4, 2 * K, G, E), BF16),
            pltpu.VMEM((HALF, HALF), BF16),
            pltpu.VMEM((G, E), F32),
            pltpu.VMEM((H, 16, G), F32),
            pltpu.VMEM((H, NC, 8, E), F32),
            pltpu.VMEM((H, NR, 8, E), F32),
            pltpu.VMEM((H, NC, 8, E), F32),
            pltpu.VMEM((H, NR, 8, E), F32),
            pltpu.VMEM((H, NC, 8, E), F32),
            pltpu.VMEM((H, NR, 8, E), F32),
            pltpu.VMEM((16, G), F32),
            pltpu.VMEM((2, ROWS, E), F32),
            pltpu.VMEM((2, E, E), F32),
            pltpu.VMEM((2, E, E), F32),
            pltpu.VMEM((2, E, E), F32),
            pltpu.SemaphoreType.DMA((H, 4)),
            pltpu.SemaphoreType.DMA((2,)),
            pltpu.SemaphoreType.DMA((H, 2)),
            pltpu.SemaphoreType.DMA((2,)),
            pltpu.SemaphoreType.DMA((H, 2)),
            pltpu.SemaphoreType.DMA((2,)),
            pltpu.SemaphoreType.DMA((H, 2)),
            pltpu.SemaphoreType.DMA((2,)),
            pltpu.SemaphoreType.DMA((H, 2)),
            pltpu.SemaphoreType.DMA((H, 2)),
            pltpu.SemaphoreType.DMA((H, 4)),
        ],
        compiler_params=pltpu.CompilerParams(
            collective_id=0, has_side_effects=True, vmem_limit_bytes=52 * 2**20
        ),
        name="attend",
    )(query_tiles, key_tiles, value_tiles, out_grad)
    query_grad, key_grad, value_grad, attended = pl.pallas_call(
        add_kernel,
        out_shape=(out,) * 4,
        in_specs=[any_spec] * 6,
        out_specs=(any_spec,) * 4,
        scratch_shapes=[
            pltpu.VMEM((4, ROWS, COLS, E), BF16),
            pltpu.VMEM((4, COLS, ROWS, E), BF16),
            pltpu.VMEM((4, ROWS, COLS, (H - 1) * E), BF16),
            pltpu.VMEM((HALF, HALF), BF16),
            pltpu.SemaphoreType.DMA((2,)),
            pltpu.SemaphoreType.DMA((4,)),
            pltpu.SemaphoreType.DMA((4, MOVES)),
            pltpu.SemaphoreType.DMA((4, MOVES)),
        ],
        compiler_params=pltpu.CompilerParams(vmem_limit_bytes=60 * 2**20),
        name="add_parts",
    )(*returned)
    return attended, query_grad, key_grad, value_grad


def solution(mesh):
    spec = P("row", "col", None)
    return jax.shard_map(
        shards, mesh=mesh, in_specs=(spec,) * 4, out_specs=(spec,) * 4, check_vma=False
    )
```

```python
import functools

import jax
import jax.numpy as jnp
from jax import lax
from jax.experimental import pallas as pl
from jax.experimental.pallas import tpu as pltpu
from jax.sharding import PartitionSpec as P

H = 4
E = 128
G = 512
ROWS = 32
COLS = 64
NR = 16
NC = 8
K = 4
HALF = 256
LOG2E = 1.4426950408889634
SCALE = E ** (-0.5)
NEG = -1e30
MOVES = 1
MESH = pl.DeviceIdType.MESH
F32 = jnp.float32
BF16 = jnp.bfloat16


def dot_nn(a, b):
    return lax.dot_general(a, b, (((1,), (0,)), ((), ())), preferred_element_type=F32)


def dot_nt(a, b):
    return lax.dot_general(a, b, (((1,), (1,)), ((), ())), preferred_element_type=F32)


def dot_tn(a, b):
    return lax.dot_general(a, b, (((0,), (0,)), ((), ())), preferred_element_type=F32)


def swap_matrix():
    to = lax.broadcasted_iota(jnp.int32, (HALF, HALF), 0)
    of = lax.broadcasted_iota(jnp.int32, (HALF, HALF), 1)
    match = of == (to % 16) * 16 + to // 16
    return jnp.where(match, 1.0, 0.0).astype(BF16)


def kernel(
    q_in, k_in, v_in, g_in, row_back, col_back, q_sum, k_sum, v_sum, o_sum,
    xs, xt, ab, perm, st, so, rs, cs, mr, mc, rr, cr, mm, pr, pc, ct, lt,
    load_sem, in_send, in_recv, out_send, out_recv, stat_send, stat_recv, merged_send, merged_recv,
    back_sem, sum_sem,
):
    me_r = lax.axis_index("row")
    me_c = lax.axis_index("col")
    core = lax.rem(me_c, 2)
    me_z = lax.rem(me_r, 4)
    inputs = (q_in, k_in, v_in, g_in)

    def row_peer(d):
        return lax.rem(me_c + d, NC)

    def col_peer(d):
        return lax.rem(me_r + d, NR)

    def load(h):
        return [
            pltpu.make_async_copy(
                inputs[a].at[:, :, pl.ds(pl.multiple_of(h * E, E), E)], xs.at[h, a], load_sem.at[h, a]
            )
            for a in range(4)
        ]

    def turn(h, a):
        for cb in range(COLS // 16):
            for rb in range(ROWS // 16):
                block = xs[h, a, rb * 16:rb * 16 + 16, cb * 16:cb * 16 + 16, :]
                moved = dot_nn(perm[...], block.reshape(HALF, E)).astype(BF16)
                xt[h, a, cb * 16:cb * 16 + 16, rb * 16:rb * 16 + 16, :] = moved.reshape(16, 16, E)

    for copy in load(0):
        copy.start()

    barrier = pltpu.get_barrier_semaphore()

    @pl.loop(1, NC)
    def _(d):
        pl.semaphore_signal(barrier, inc=1, device_id=(me_r, row_peer(d)), device_id_type=MESH)

    @pl.loop(1, NR)
    def _(d):
        pl.semaphore_signal(barrier, inc=1, device_id=(col_peer(d), me_c), device_id_type=MESH)

    perm[...] = swap_matrix()
    st[...] = jnp.zeros_like(st)
    lt[...] = jnp.zeros_like(lt)
    first_load = load(0)
    first_load[0].wait()
    turn(0, 0)
    for copy in first_load[1:]:
        copy.wait()
    pl.semaphore_wait(barrier, NC + NR - 2)

    def send_in(h):
        @pl.when(h > 0)
        def _():
            for copy in load(h):
                copy.wait()

        @pl.when(h < H - 1)
        def _():
            for copy in load(h + 1):
                copy.start()

        def row_src(dst):
            return xs.at[h, :, pl.ds(dst * K, K)]

        row_dst = ab.at[h, :, pl.ds(0, K), pl.ds(pl.multiple_of(me_c * COLS, COLS), COLS)]

        @pl.loop(0, 4)
        def _(a):
            @pl.when(h + a > 0)
            def _():
                turn(h, a)

            def col_src(dst):
                return xt.at[h, a, pl.ds(dst * K, K)]

            col_dst = ab.at[h, a, pl.ds(K, K), pl.ds(pl.multiple_of(me_r * ROWS, ROWS), ROWS)]

            @pl.loop(1, NR)
            def _(d):
                dst = col_peer(d)
                pltpu.make_async_remote_copy(
                    src_ref=col_src(dst), dst_ref=col_dst, send_sem=in_send.at[1], recv_sem=in_recv.at[h, 1],
                    device_id=(dst, me_c), device_id_type=MESH,
                ).start()

            pltpu.make_async_copy(col_src(me_r), col_dst, in_recv.at[h, 1]).start()

            @pl.when(a == 0)
            def _():
                @pl.loop(1, NC)
                def _(d):
                    dst = row_peer(d)
                    pltpu.make_async_remote_copy(
                        src_ref=row_src(dst), dst_ref=row_dst, send_sem=in_send.at[0], recv_sem=in_recv.at[h, 0],
                        device_id=(me_r, dst), device_id_type=MESH,
                    ).start()

                pltpu.make_async_copy(row_src(me_c), row_dst, in_recv.at[h, 0]).start()

    def forward(h):
        lane = lax.broadcasted_iota(jnp.int32, (HALF, E), 1)
        q_pos = lax.broadcasted_iota(jnp.int32, (HALF, HALF), 0)
        k_pos = lax.broadcasted_iota(jnp.int32, (HALF, HALF), 1)

        for part in range(2):
            here = ab.at[h, :, pl.ds(part * K, K)]
            pltpu.make_async_copy(here, here, in_recv.at[h, part]).wait()

            @pl.loop(0, K)
            def _(k):
                i = part * K + k
                allowed = k_pos <= q_pos - part
                for qb in range(2):
                    rows = pl.ds(qb * HALF, HALF)
                    query = ab[h, 0, i, rows, :]
                    scores = [
                        dot_nt(query, ab[h, 1, i, pl.ds(kb * HALF, HALF), :]) * (SCALE * LOG2E)
                        for kb in range(qb + 1)
                    ]
                    scores[qb] = jnp.where(allowed, scores[qb], NEG)
                    top = scores[0].max(axis=-1, keepdims=True)
                    for s in scores[1:]:
                        top = jnp.maximum(top, s.max(axis=-1, keepdims=True))
                    top = jnp.maximum(top, 0.1 * NEG)
                    weights = [jnp.exp2(s - top) for s in scores]
                    total = weights[0].sum(axis=-1, keepdims=True)
                    for w in weights[1:]:
                        total = total + w.sum(axis=-1, keepdims=True)
                    total = jnp.maximum(total, 1.0)
                    numer = dot_nn(weights[0].astype(BF16), ab[h, 2, i, pl.ds(0, HALF), :])
                    if qb:
                        numer = numer + dot_nn(weights[1].astype(BF16), ab[h, 2, i, pl.ds(HALF, HALF), :])
                    out = (numer / total).astype(BF16).astype(F32)
                    product = (ab[h, 3, i, rows, :].astype(F32) * out).sum(axis=-1, keepdims=True)
                    log_part = top + jnp.log2(total)
                    base = part * 8 + k
                    st[rows, :] = jnp.where(
                        lane == base, log_part, jnp.where(lane == base + 4, product, st[rows, :])
                    )

        for b in range(4):
            block = st[b * E:(b + 1) * E, :].T
            so[h, :, b * E:(b + 1) * E] = block[:16, :]

        def row_stat(dst):
            return so.at[h, pl.ds(0, 8), pl.ds(pl.multiple_of((dst // 2) * E, E), E)]

        def col_stat(dst):
            return so.at[h, pl.ds(8, 8), pl.ds(pl.multiple_of((dst // 4) * E, E), E)]

        @pl.loop(1, NC)
        def _(d):
            dst = row_peer(d)
            pltpu.make_async_remote_copy(
                src_ref=row_stat(dst), dst_ref=rs.at[h, me_c], send_sem=stat_send.at[0],
                recv_sem=stat_recv.at[h, 0], device_id=(me_r, dst), device_id_type=MESH,
            ).start()

        pltpu.make_async_copy(row_stat(me_c), rs.at[h, me_c], stat_recv.at[h, 0]).start()

        @pl.loop(1, NR)
        def _(d):
            dst = col_peer(d)
            pltpu.make_async_remote_copy(
                src_ref=col_stat(dst), dst_ref=cs.at[h, me_r], send_sem=stat_send.at[1],
                recv_sem=stat_recv.at[h, 1], device_id=(dst, me_c), device_id_type=MESH,
            ).start()

        pltpu.make_async_copy(col_stat(me_r), cs.at[h, me_r], stat_recv.at[h, 1]).start()

    def merge(h):
        pltpu.make_async_copy(rs.at[h], rs.at[h], stat_recv.at[h, 0]).wait()
        pltpu.make_async_copy(cs.at[h], cs.at[h], stat_recv.at[h, 1]).wait()
        row_values = []
        col_values = []
        for s in range(2):
            for d in range(NC):
                pr[s, 4 * d:4 * d + 4, :] = rs[h, d, 4 * s:4 * s + 4, :]
            for j in range(NR):
                pc[s, 4 * j:4 * j + 4, :] = cs[h, j, 4 * s:4 * s + 4, :]
                pc[s, COLS + 4 * j:COLS + 4 * j + 4, :] = cs[h, j, 4 * s:4 * s + 4, :]
            ct[s] = pc[s].T
            row_values.append(pr[s])
            col_values.append(ct[s, pl.ds(pl.multiple_of(me_z * ROWS, ROWS), ROWS), :])
        top = jnp.maximum(row_values[0], col_values[0])
        log_total = top + jnp.log2(jnp.exp2(row_values[0] - top) + jnp.exp2(col_values[0] - top))
        delta = (
            jnp.exp2(row_values[0] - log_total) * row_values[1]
            + jnp.exp2(col_values[0] - log_total) * col_values[1]
        )
        for s, value in enumerate((log_total, delta)):
            pr[s] = value
            lt[s, pl.ds(pl.multiple_of(me_z * ROWS, ROWS), ROWS), :] = value
            turned = lt[s].T
            pc[s, :COLS, :] = jnp.where(core == 0, turned[:COLS], turned[COLS:])
            for d in range(NC):
                mr[h, d, 4 * s:4 * s + 4, :] = pr[s, 4 * d:4 * d + 4, :]
            for j in range(NR):
                mc[h, j, 4 * s:4 * s + 4, :] = pc[s, 4 * j:4 * j + 4, :]

        @pl.loop(1, NC)
        def _(d):
            dst = row_peer(d)
            pltpu.make_async_remote_copy(
                src_ref=mr.at[h, dst], dst_ref=rr.at[h, me_c], send_sem=merged_send.at[0],
                recv_sem=merged_recv.at[h, 0], device_id=(me_r, dst), device_id_type=MESH,
            ).start()

        pltpu.make_async_copy(mr.at[h, me_c], rr.at[h, me_c], merged_recv.at[h, 0]).start()

        @pl.loop(1, NR)
        def _(d):
            dst = col_peer(d)
            pltpu.make_async_remote_copy(
                src_ref=mc.at[h, dst], dst_ref=cr.at[h, me_r], send_sem=merged_send.at[1],
                recv_sem=merged_recv.at[h, 1], device_id=(dst, me_c), device_id_type=MESH,
            ).start()

        pltpu.make_async_copy(mc.at[h, me_r], cr.at[h, me_r], merged_recv.at[h, 1]).start()

    def backward(h):
        pltpu.make_async_copy(rr.at[h], rr.at[h], merged_recv.at[h, 0]).wait()
        pltpu.make_async_copy(cr.at[h], cr.at[h], merged_recv.at[h, 1]).wait()
        lane = lax.broadcasted_iota(jnp.int32, (8, E), 1)
        for y in range(4):
            mm[0:8, y * E:(y + 1) * E] = jnp.where(lane < COLS, rr[h, 2 * y], rr[h, 2 * y + 1])
            tile = cr[h, 4 * y]
            for z in range(1, 4):
                tile = jnp.where(lane >= z * ROWS, cr[h, 4 * y + z], tile)
            mm[8:16, y * E:(y + 1) * E] = tile

        k_pos = lax.broadcasted_iota(jnp.int32, (HALF, HALF), 0)
        q_pos = lax.broadcasted_iota(jnp.int32, (HALF, HALF), 1)

        def instance(part, k):
            i = part * K + k
            allowed = k_pos <= q_pos - part
            key_grads = [None, None]
            value_grads = [None, None]
            for qb in range(2):
                rows = pl.ds(qb * HALF, HALF)
                query = ab[h, 0, i, rows, :]
                grad = ab[h, 3, i, rows, :]
                log_total = mm[pl.ds(part * 8 + k, 1), rows]
                delta = mm[pl.ds(part * 8 + 4 + k, 1), rows]
                query_grad = None
                out = None
                for kb in range(qb + 1):
                    keys = ab[h, 1, i, pl.ds(kb * HALF, HALF), :]
                    values = ab[h, 2, i, pl.ds(kb * HALF, HALF), :]
                    scores = dot_nt(keys, query) * (SCALE * LOG2E)
                    if kb == qb:
                        scores = jnp.where(allowed, scores, NEG)
                    probs = jnp.exp2(scores - log_total)
                    score_grad = probs * (dot_nt(values, grad) - delta)
                    probs_half = probs.astype(BF16)
                    score_half = score_grad.astype(BF16)
                    terms = (
                        dot_nn(score_half, query), dot_nn(probs_half, grad),
                        dot_tn(keys, score_half), dot_tn(values, probs_half),
                    )
                    if kb < qb:
                        key_grads[kb] = key_grads[kb] + terms[0]
                        value_grads[kb] = value_grads[kb] + terms[1]
                    else:
                        key_grads[kb] = terms[0]
                        value_grads[kb] = terms[1]
                    query_grad = terms[2] if query_grad is None else query_grad + terms[2]
                    out = terms[3] if out is None else out + terms[3]
                ab[h, 0, i, rows, :] = (query_grad * SCALE).T.astype(BF16)
                ab[h, 3, i, rows, :] = out.T.astype(BF16)
            for kb in range(2):
                where = pl.ds(kb * HALF, HALF)
                ab[h, 1, i, where, :] = (key_grads[kb] * SCALE).astype(BF16)
                ab[h, 2, i, where, :] = value_grads[kb].astype(BF16)

        @pl.loop(0, K)
        def _(k):
            instance(1, k)

            def col_src(dst):
                return ab.at[h, :, K + k, pl.ds(pl.multiple_of(dst * ROWS, ROWS), ROWS)]

            col_dst = col_back.at[h, :, me_r * K + k]

            @pl.loop(1, NR)
            def _(d):
                dst = col_peer(d)
                pltpu.make_async_remote_copy(
                    src_ref=col_src(dst), dst_ref=col_dst, send_sem=out_send.at[1],
                    recv_sem=out_recv.at[h, 1], device_id=(dst, me_c), device_id_type=MESH,
                ).start()

            pltpu.make_async_copy(col_src(me_r), col_dst, out_recv.at[h, 1]).start()
            instance(0, k)

            def row_src(dst):
                return ab.at[h, :, k, pl.ds(pl.multiple_of(dst * COLS, COLS), COLS)]

            row_dst = row_back.at[h, :, me_c * K + k]

            @pl.loop(1, NC)
            def _(d):
                dst = row_peer(d)
                pltpu.make_async_remote_copy(
                    src_ref=row_src(dst), dst_ref=row_dst, send_sem=out_send.at[0],
                    recv_sem=out_recv.at[h, 0], device_id=(me_r, dst), device_id_type=MESH,
                ).start()

            pltpu.make_async_copy(row_src(me_c), row_dst, out_recv.at[h, 0]).start()

    send_in(0)
    send_in(1)

    @pl.loop(0, H + 2)
    def _(t):
        @pl.when(t < H)
        def _():
            forward(t)

        @pl.when(t < H - 2)
        def _():
            send_in(t + 2)

        @pl.when(jnp.logical_and(t >= 1, t <= H))
        def _():
            merge(t - 1)

        @pl.when(t >= 2)
        def _():
            backward(t - 2)

    def drain(ref, sem):
        pltpu.make_async_copy(ref, ref, sem).wait()

    row_sent = ab.at[:, :, pl.ds(0, K), pl.ds(0, G - COLS)]
    col_sent = ab.at[:, :, pl.ds(0, K), pl.ds(0, G - ROWS)]
    drain(row_sent, in_send.at[0])
    drain(col_sent, in_send.at[1])

    sums = (q_sum, k_sum, v_sum, o_sum)

    def store(h, a):
        return pltpu.make_async_copy(xs.at[h, a], sums[a].at[:, :, h * E:(h + 1) * E], sum_sem.at[h, a])

    for h in range(H - 1):
        drain(row_back.at[h], out_recv.at[h, 0])
        drain(col_back.at[h], out_recv.at[h, 1])
        backs = [
            pltpu.make_async_copy(row_back.at[h], xs.at[h], back_sem.at[h, 0]),
            pltpu.make_async_copy(col_back.at[h], xt.at[h], back_sem.at[h, 1]),
        ]
        for copy in backs:
            copy.start()
        for copy in backs:
            copy.wait()

        @pl.loop(0, COLS // 16)
        def _(cb):
            add_block(perm, xs.at[h], xt.at[h], xs.at[h], cb)

        for a in range(4):
            store(h, a).start()

    for h in range(H - 1):
        for a in range(4):
            store(h, a).wait()
    drain(row_sent, out_send.at[0])
    drain(col_sent, out_send.at[1])
    drain(rs.at[:, pl.ds(0, NC - 1)], stat_send.at[0])
    drain(cs.at[:, pl.ds(0, NR - 1)], stat_send.at[1])
    drain(rr.at[:, pl.ds(0, NC - 1)], merged_send.at[0])
    drain(cr.at[:, pl.ds(0, NR - 1)], merged_send.at[1])
    drain(row_back.at[H - 1], out_recv.at[H - 1, 0])
    drain(col_back.at[H - 1], out_recv.at[H - 1, 1])


def add_block(perm, first, second, total, cb):
    cols = pl.ds(cb * 16 if isinstance(cb, int) else pl.multiple_of(cb * 16, 16), 16)
    for rb in range(ROWS // 16):
        rows = pl.ds(rb * 16, 16)
        for a in range(0, 4, 2):
            pair = [second[a + n, cols, rows, :].reshape(HALF, E) for n in range(2)]
            moved = dot_nn(perm[...], jnp.concatenate(pair, axis=1))
            for n in range(2):
                mine = first[a + n, rows, cols, :].reshape(HALF, E).astype(F32)
                both = (mine + moved[:, n * E:(n + 1) * E]).astype(BF16)
                total[a + n, rows, cols, :] = both.reshape(16, 16, E)


def add_kernel(
    row_back, col_back, q_sum, k_sum, v_sum, o_sum, q_out, k_out, v_out, o_out,
    first, second, stage, perm, back_sem, out_sem, load_sem, store_sem,
):
    sums = (q_sum, k_sum, v_sum, o_sum)
    outs = (q_out, k_out, v_out, o_out)
    backs = [
        pltpu.make_async_copy(row_back.at[H - 1], first, back_sem.at[0]),
        pltpu.make_async_copy(col_back.at[H - 1], second, back_sem.at[1]),
    ]
    for copy in backs:
        copy.start()
    loads = []
    stores = []
    for n in range(MOVES):
        for a in range(4):
            part = (pl.ds(n * (ROWS // MOVES), ROWS // MOVES), slice(None), pl.ds(0, (H - 1) * E))
            here = stage.at[(a,) + part[:2]]
            loads.append(pltpu.make_async_copy(sums[a].at[part], here, load_sem.at[a, n]))
            stores.append(pltpu.make_async_copy(here, outs[a].at[part], store_sem.at[a, n]))
    for copy in loads:
        copy.start()
    perm[...] = swap_matrix()
    for copy in backs:
        copy.wait()
    step = len(loads) // (COLS // 16)
    for cb in range(COLS // 16):
        add_block(perm, first, second, first, cb)
        for n in range(cb * step, cb * step + step):
            loads[n].wait()
            stores[n].start()
    last = [
        pltpu.make_async_copy(first.at[a], outs[a].at[:, :, pl.ds((H - 1) * E, E)], out_sem.at[a])
        for a in range(4)
    ]
    for copy in last:
        copy.start()
    for copy in last + stores:
        copy.wait()


def shards(query_tiles, key_tiles, value_tiles, out_grad):
    any_spec = pl.BlockSpec(memory_space=pl.ANY)
    out = jax.ShapeDtypeStruct((ROWS, COLS, H * E), BF16)
    backs = (
        jax.ShapeDtypeStruct((H, 4, ROWS, COLS, E), BF16),
        jax.ShapeDtypeStruct((H, 4, COLS, ROWS, E), BF16),
    )
    returned = pl.pallas_call(
        kernel,
        out_shape=backs + (out,) * 4,
        in_specs=[any_spec] * 4,
        out_specs=(any_spec,) * 6,
        scratch_shapes=[
            pltpu.VMEM((H, 4, ROWS, COLS, E), BF16),
            pltpu.VMEM((H, 4, COLS, ROWS, E), BF16),
            pltpu.VMEM((H, 4, 2 * K, G, E), BF16),
            pltpu.VMEM((HALF, HALF), BF16),
            pltpu.VMEM((G, E), F32),
            pltpu.VMEM((H, 16, G), F32),
            pltpu.VMEM((H, NC, 8, E), F32),
            pltpu.VMEM((H, NR, 8, E), F32),
            pltpu.VMEM((H, NC, 8, E), F32),
            pltpu.VMEM((H, NR, 8, E), F32),
            pltpu.VMEM((H, NC, 8, E), F32),
            pltpu.VMEM((H, NR, 8, E), F32),
            pltpu.VMEM((16, G), F32),
            pltpu.VMEM((2, ROWS, E), F32),
            pltpu.VMEM((2, E, E), F32),
            pltpu.VMEM((2, E, E), F32),
            pltpu.VMEM((2, E, E), F32),
            pltpu.SemaphoreType.DMA((H, 4)),
            pltpu.SemaphoreType.DMA((2,)),
            pltpu.SemaphoreType.DMA((H, 2)),
            pltpu.SemaphoreType.DMA((2,)),
            pltpu.SemaphoreType.DMA((H, 2)),
            pltpu.SemaphoreType.DMA((2,)),
            pltpu.SemaphoreType.DMA((H, 2)),
            pltpu.SemaphoreType.DMA((2,)),
            pltpu.SemaphoreType.DMA((H, 2)),
            pltpu.SemaphoreType.DMA((H, 2)),
            pltpu.SemaphoreType.DMA((H, 4)),
        ],
        compiler_params=pltpu.CompilerParams(
            collective_id=0, has_side_effects=True, vmem_limit_bytes=52 * 2**20
        ),
        name="attend",
    )(query_tiles, key_tiles, value_tiles, out_grad)
    query_grad, key_grad, value_grad, attended = pl.pallas_call(
        add_kernel,
        out_shape=(out,) * 4,
        in_specs=[any_spec] * 6,
        out_specs=(any_spec,) * 4,
        scratch_shapes=[
            pltpu.VMEM((4, ROWS, COLS, E), BF16),
            pltpu.VMEM((4, COLS, ROWS, E), BF16),
            pltpu.VMEM((4, ROWS, COLS, (H - 1) * E), BF16),
            pltpu.VMEM((HALF, HALF), BF16),
            pltpu.SemaphoreType.DMA((2,)),
            pltpu.SemaphoreType.DMA((4,)),
            pltpu.SemaphoreType.DMA((4, MOVES)),
            pltpu.SemaphoreType.DMA((4, MOVES)),
        ],
        compiler_params=pltpu.CompilerParams(vmem_limit_bytes=60 * 2**20),
        name="add_parts",
    )(*returned)
    return attended, query_grad, key_grad, value_grad


def solution(mesh):
    spec = P("row", "col", None)
    return jax.shard_map(
        shards, mesh=mesh, in_specs=(spec,) * 4, out_specs=(spec,) * 4, check_vma=False
    )
```
